256 devices in a mesh: wide: 64 (over y, x_lo, z), narrow: 4 (over x_hi, core).
Axes of the slice: x: 4 (x_hi: 2, x_lo: 2; x = x_hi * 2 + x_lo), y: 4, z: 8, core: 2. Of those that a mesh axis runs over, the one named last changes fastest.
Arguments:
- gradient: bfloat16 [2560, 7168], P('wide', 'narrow'), may hold values from -6 to 6
- left_basis: bfloat16 [2560, 2560], P(None, 'narrow'), may hold values from -0.125 to 0.125
- right_basis: bfloat16 [7168, 7168], P('wide', 'narrow'), may hold values from -0.0625 to 0.0625
- first_moment: float32 [7168, 2560], P('wide', 'narrow'), may hold values from -0.6 to 0.6
- second_moment: float32 [7168, 2560], P('wide', 'narrow'), may hold values from 0.01 to 0.1
Outputs:
- update: float32 [2560, 7168], P('wide', 'narrow')
- new_first: float32 [7168, 2560], P('wide', 'narrow')
- new_second: float32 [7168, 2560], P('wide', 'narrow')
The draws below stay inside these ranges and needn't reach their ends.
All inputs are finite; a program needn't handle non-finite values.
Results may differ from the reference program's by a relative error of at most 0.0038.
Values may be sent and summed in bfloat16 or wider, within the bound.
A program may use at most 64 MiB of HBM per device.

```python
import math
import jax
import jax.numpy as jnp

M = 2560
N = 7168
STEP = 10


def levels(own_key, shape, split, least, top_value):
    level, own = 1.0, jax.random.fold_in(own_key, 6)
    for axis_at, blocks in split:
        heights = jnp.exp(jax.random.uniform(jax.random.fold_in(own, axis_at), (blocks,), jnp.float32, least / len(split), top_value / len(split)))
        level = level * jnp.repeat(heights, shape[axis_at] // blocks).reshape([-1 if axis == axis_at else 1 for axis in range(len(shape))])
    return level


def normal_values(rng, shape, width, reach, cuts=(), dtype=jnp.bfloat16):
    values = jax.random.normal(rng, shape, jnp.float32) * width
    if len(cuts) > 0:
        values = levels(rng, shape, cuts, -0.22, 0.18) * values
    return jnp.clip(values, min=-reach, max=reach).astype(dtype)


def setup_inputs(seed: int = 0) -> dict:
    streams_of = jax.random.split(jax.random.key(seed), 6)
    return {
        "gradient": normal_values(streams_of[0], (M, N), 1.0, 6.0, ((0, 64), (1, 4))),
        "left_basis": normal_values(streams_of[1], (M, M), M ** -0.5, 0.125, ((1, 4),)),
        "right_basis": normal_values(streams_of[2], (N, N), N ** -0.5, 0.0625, ((0, 64), (1, 4))),
        "first_moment": normal_values(streams_of[3], (N, M), 0.1, 0.6, ((0, 64), (1, 4)), jnp.float32),
        "second_moment": jnp.clip(jnp.exp(math.log(0.1) - 2.3025851 * jax.random.uniform(streams_of[4], (N, M), jnp.float32) ** levels(streams_of[4], (N, M), ((0, 64), (1, 4)), -0.2, 0.2)), 0.01, 0.1),
    }


beta_first = 0.9
beta_second = 0.95
epsilon = 1e-08

def reference(gradient, left_basis, right_basis, first_moment, second_moment):
    right_rotated = jnp.dot(right_basis, gradient.T, preferred_element_type=jnp.float32).astype(jnp.bfloat16)
    rotated = jnp.dot(right_rotated, left_basis, preferred_element_type=jnp.float32)
    new_first = beta_first * first_moment + (1.0 - beta_first) * rotated
    new_second = beta_second * second_moment + (1.0 - beta_second) * rotated * rotated
    first_fix = 1.0 - beta_first ** STEP
    second_fix = 1.0 - beta_second ** STEP
    normalized = (new_first / first_fix / (jnp.sqrt(new_second / second_fix) + epsilon)).astype(jnp.bfloat16)
    back_left = jnp.dot(normalized, left_basis.T, preferred_element_type=jnp.float32).astype(jnp.bfloat16)
    update = jnp.dot(back_left.T, right_basis, preferred_element_type=jnp.float32)
    return (update, new_first, new_second)
```

```python
import functools

import jax
import jax.numpy as jnp
from jax import lax
from jax.experimental import pallas as pl
from jax.experimental.pallas import tpu as pltpu
from jax.sharding import PartitionSpec as P

STEP = 10

beta_first = 0.9
beta_second = 0.95
epsilon = 1e-08

MESH = pl.DeviceIdType.MESH
BF16 = jnp.bfloat16
F32 = jnp.float32

NY, NXL, NZ = 4, 2, 8
GROUP = NY * NXL
GROWS = 40
ROWS = 112
COLS = 1792
EIG = 640
BLOCK = NZ * GROWS
HALF = COLS // 2
PART = 64
OFFSET = ROWS - PART
ORDER = ((0, 0), (0, 1), (1, 0), (3, 0), (2, 0), (1, 1), (3, 1), (2, 1))
TOP, LOW = (0, 64), (64, 48)


class Copies:
    def __init__(self, send_sem, recv_sem):
        self.send_sem, self.recv_sem, self.made = send_sem, recv_sem, {}

    def start(self, name, src, dst, device):
        at = len(self.made)
        copy = pltpu.make_async_remote_copy(
            src_ref=src,
            dst_ref=dst,
            send_sem=self.send_sem.at[at],
            recv_sem=self.recv_sem.at[at],
            device_id=device,
            device_id_type=MESH,
        )
        copy.start()
        self.made[name] = copy

    def wait(self, name):
        self.made[name].wait_recv()

    def finish(self):
        for copy in self.made.values():
            copy.wait_send()


def kernel(
    gradient, left_basis, right_basis, first_moment, second_moment,
    update, new_first, new_second,
    g_slots, g_wide, g_all, r_slots, left, first, second, first_out, second_out,
    forward, forward_got, forward_sent, forward_in, rotated_in,
    back, back_got, back_sent, back_in, back_left,
    total, sums, sums_in, update_out,
    local_sem, send_sem, recv_sem,
):
    wide, narrow = lax.axis_index("wide"), lax.axis_index("narrow")
    y, xl, z = wide // (NXL * NZ), lax.rem(wide // NZ, NXL), lax.rem(wide, NZ)
    xh, core = narrow // 2, lax.rem(narrow, 2)
    own = wide // NZ

    def member(dy, dxl):
        return lax.rem(y + dy, NY) * NXL + lax.rem(xl + dxl, NXL)

    def at(group=own, zz=z, hi=xh, cc=core):
        return {"wide": group * NZ + zz, "narrow": hi * 2 + cc}

    z_up, z_down = at(zz=lax.rem(z + 1, NZ)), at(zz=lax.rem(z + NZ - 1, NZ))
    y_up, y_down = at(group=member(1, 0)), at(group=member(3, 0))
    x_other = at(group=member(0, 1))
    sibling = at(cc=1 - core)
    hi_other = 1 - xh

    loads = [
        pltpu.make_async_copy(src, dst, local_sem.at[i])
        for i, (src, dst) in enumerate(
            (
                (gradient, g_slots.at[z]),
                (right_basis, r_slots.at[own]),
                (left_basis, left),
                (first_moment, first),
                (second_moment, second),
            )
        )
    ]
    for load in loads:
        load.start()

    barrier = pltpu.get_barrier_semaphore()
    peers = [z_up, z_down, sibling]
    for dy, dxl in ORDER:
        for hi in (xh, hi_other):
            if (dy, dxl) != (0, 0) or hi is not xh:
                peers.append(at(group=member(dy, dxl), hi=hi))
    for peer in peers:
        pl.semaphore_signal(barrier, inc=1, device_id=peer, device_id_type=MESH)
    pl.semaphore_wait(barrier, len(peers))

    copies = Copies(send_sem, recv_sem)

    def g_slot(distance):
        return g_slots.at[lax.rem(z + distance + NZ, NZ)]

    def g_piece(distance, half):
        return g_slots.at[lax.rem(z + distance + NZ, NZ), :, pl.ds(half * HALF, HALF)]

    def r_piece(dy, dxl, piece):
        return r_slots.at[member(dy, dxl), pl.ds(*piece), :]

    def send_r(name, dy, dxl, piece, device):
        ref = r_piece(dy, dxl, piece)
        copies.start(name, ref, ref, device)

    loads[0].wait()
    copies.start("g+1", g_slot(0), g_slot(0), z_up)
    copies.start("g-1", g_slot(0), g_slot(0), z_down)
    loads[1].wait()
    for tag, piece in (("t", TOP), ("l", LOW)):
        send_r("y+" + tag, 0, 0, piece, y_up)
        send_r("y-" + tag, 0, 0, piece, y_down)
        send_r("x" + tag, 0, 0, piece, x_other)
    for hop in (1,):
        copies.wait("g+1")
        copies.start("g+2", g_slot(-1), g_slot(-1), z_up)
        copies.wait("g-1")
        copies.start("g-2", g_slot(1), g_slot(1), z_down)
    copies.wait("y+t")
    send_r("yy+", 3, 0, TOP, y_up)
    send_r("xt3", 3, 0, TOP, x_other)
    copies.wait("y-t")
    send_r("xt1", 1, 0, TOP, x_other)
    copies.wait("g+2")
    copies.start("g+3", g_slot(-2), g_slot(-2), z_up)
    copies.wait("g-2")
    copies.start("g-3", g_slot(2), g_slot(2), z_down)
    copies.wait("y-l")
    send_r("yy-", 1, 0, LOW, y_down)
    copies.wait("xl")
    send_r("yx+", 0, 1, LOW, y_up)
    send_r("yx-", 0, 1, LOW, y_down)
    copies.wait("g+3")
    copies.start("g+4", g_piece(-3, 0), g_piece(-3, 0), z_up)
    copies.wait("g-3")
    copies.start("g-4", g_piece(3, 1), g_piece(3, 1), z_down)
    copies.wait("yx+")
    send_r("yxx+", 3, 1, LOW, y_up)
    copies.wait("xt1")
    send_r("yxx-", 1, 1, TOP, y_down)
    copies.wait("g+4")
    copies.wait("g-4")

    for i in range(NZ):
        g_wide[pl.ds(i * GROWS, GROWS), :] = g_slots[i].astype(F32)
    g_all[...] = g_wide[...].astype(BF16)

    needs = {
        (0, 0): (),
        (0, 1): ("xt",),
        (1, 0): (),
        (3, 0): ("y+l",),
        (2, 0): ("yy+", "yy-"),
        (1, 1): ("yx-",),
        (3, 1): ("xt3",),
        (2, 1): ("yxx+", "yxx-"),
    }

    mine = pl.ds(pl.multiple_of(core * OFFSET, 16), PART)
    theirs = pl.ds(pl.multiple_of((1 - core) * OFFSET, 16), PART)
    kept = pl.ds(pl.multiple_of(core * PART, 16), OFFSET)

    def give_core(tag, partial, got, group):
        copies.start(tag, partial.at[group, theirs, :], got.at[group], sibling)

    def spread(tag, partial, got, sent, landed):
        for dy, dxl in ORDER:
            group = member(dy, dxl)
            copies.wait(f"{tag}c{dy}{dxl}")
            sent[group] = (partial[group, mine, :] + got[group]).astype(BF16)
            for e, hi in ((0, xh), (1, hi_other)):
                if (dy, dxl, e) != (0, 0, 0):
                    copies.start(
                        f"{tag}s{dy}{dxl}{e}", sent.at[group], landed.at[e, own], at(group=group, hi=hi)
                    )

    def collect(tag, sent, landed, result):
        for dy, dxl in ORDER:
            source = member((NY - dy) % NY, dxl)
            if (dy, dxl) == (0, 0):
                here = sent[own]
            else:
                copies.wait(f"{tag}s{dy}{dxl}0")
                here = landed[0, source]
            copies.wait(f"{tag}s{dy}{dxl}1")
            result[source, mine, :] = (here.astype(F32) + landed[1, source].astype(F32)).astype(BF16)
            ref = result.at[source, kept, :]
            copies.start(f"{tag}r{dy}{dxl}", ref, ref, sibling)

    for dy, dxl in ORDER:
        for name in needs[(dy, dxl)]:
            copies.wait(name)
        group = member(dy, dxl)
        forward[group] = lax.dot_general(
            r_slots[group], g_all[...], (((1,), (1,)), ((), ())), preferred_element_type=F32
        )
        give_core(f"fc{dy}{dxl}", forward, forward_got, group)
    spread("f", forward, forward_got, forward_sent, forward_in)
    collect("f", forward_sent, forward_in, rotated_in)

    loads[2].wait()

    def left_rows(group):
        return left[pl.ds(pl.multiple_of(group * BLOCK, 64), BLOCK), :]

    rotated = jnp.zeros((ROWS, EIG), F32)
    for dy, dxl in ORDER:
        source = member((NY - dy) % NY, dxl)
        copies.wait(f"fr{dy}{dxl}")
        rotated += jnp.dot(rotated_in[source], left_rows(source), preferred_element_type=F32)

    loads[3].wait()
    loads[4].wait()
    next_first = beta_first * first[...] + (1.0 - beta_first) * rotated
    next_second = beta_second * second[...] + (1.0 - beta_second) * rotated * rotated
    first_out[...] = next_first
    second_out[...] = next_second
    stores = [
        pltpu.make_async_copy(first_out, new_first, local_sem.at[5]),
        pltpu.make_async_copy(second_out, new_second, local_sem.at[6]),
    ]
    for store in stores:
        store.start()
    first_fix = 1.0 - beta_first**STEP
    second_fix = 1.0 - beta_second**STEP
    normalized = (next_first / first_fix / (jnp.sqrt(next_second / second_fix) + epsilon)).astype(BF16)

    for dy, dxl in ORDER:
        group = member(dy, dxl)
        back[group] = lax.dot_general(
            normalized, left_rows(group), (((1,), (1,)), ((), ())), preferred_element_type=F32
        )
        give_core(f"bc{dy}{dxl}", back, back_got, group)
    spread("b", back, back_got, back_sent, back_in)
    collect("b", back_sent, back_in, back_left)
    for dy, dxl in ORDER:
        copies.wait(f"br{dy}{dxl}")

    total[...] = lax.dot_general(
        back_left[...].reshape(GROUP * ROWS, BLOCK),
        r_slots[...].reshape(GROUP * ROWS, COLS),
        (((0,), (0,)), ((), ())),
        preferred_element_type=F32,
    )

    def total_rows(distance, half):
        rows = lax.rem(z + distance + NZ, NZ) * GROWS
        return total[pl.ds(pl.multiple_of(rows, 8), GROWS), pl.ds(half * HALF, HALF)]

    for step in range(4):
        for way, sign, device in ((0, -1, z_down), (1, 1, z_up)):
            for half in (0, 1):
                if step == 0 and half != way:
                    continue
                value = total_rows(sign * (4 - step), half)
                if step > 1 or (step == 1 and half == way):
                    copies.wait(f"u{step - 1}{way}{half}")
                    value = value + sums_in[way, step - 1, half]
                sums[way, step, half] = value
                copies.start(f"u{step}{way}{half}", sums.at[way, step, half], sums_in.at[way, step, half], device)
    for half in (0, 1):
        value = total_rows(0, half)
        for way in (0, 1):
            copies.wait(f"u3{way}{half}")
            value = value + sums_in[way, 3, half]
        update_out[:, pl.ds(half * HALF, HALF)] = value
    last = pltpu.make_async_copy(update_out, update, local_sem.at[7])
    last.start()
    last.wait()
    for store in stores:
        store.wait()
    copies.finish()


COPIES = 8 + 14 + 2 * (8 + 15 + 8) + 14


def body(gradient, left_basis, right_basis, first_moment, second_moment):
    partials = [
        pltpu.VMEM((GROUP, ROWS, BLOCK), F32),
        pltpu.VMEM((GROUP, PART, BLOCK), F32),
        pltpu.VMEM((GROUP, PART, BLOCK), BF16),
        pltpu.VMEM((2, GROUP, PART, BLOCK), BF16),
        pltpu.VMEM((GROUP, ROWS, BLOCK), BF16),
    ]
    moment = pltpu.VMEM((ROWS, EIG), F32)
    return pl.pallas_call(
        kernel,
        out_shape=(
            jax.ShapeDtypeStruct((GROWS, COLS), F32),
            jax.ShapeDtypeStruct((ROWS, EIG), F32),
            jax.ShapeDtypeStruct((ROWS, EIG), F32),
        ),
        in_specs=[pl.BlockSpec(memory_space=pl.ANY)] * 5,
        out_specs=[pl.BlockSpec(memory_space=pl.ANY)] * 3,
        scratch_shapes=[
            pltpu.VMEM((NZ, GROWS, COLS), BF16),
            pltpu.VMEM((BLOCK, COLS), F32),
            pltpu.VMEM((BLOCK, COLS), BF16),
            pltpu.VMEM((GROUP, ROWS, COLS), BF16),
            pltpu.VMEM((GROUP * BLOCK, EIG), BF16),
            moment,
            moment,
            moment,
            moment,
            *partials,
            *partials,
            pltpu.VMEM((BLOCK, COLS), F32),
            pltpu.VMEM((2, 4, 2, GROWS, HALF), F32),
            pltpu.VMEM((2, 4, 2, GROWS, HALF), F32),
            pltpu.VMEM((GROWS, COLS), F32),
            pltpu.SemaphoreType.DMA((8,)),
            pltpu.SemaphoreType.DMA((COPIES,)),
            pltpu.SemaphoreType.DMA((COPIES,)),
        ],
        compiler_params=pltpu.CompilerParams(
            collective_id=0, has_side_effects=True, vmem_limit_bytes=56 * 1024 * 1024
        ),
        cost_estimate=pl.CostEstimate(flops=3 * 10**9, bytes_accessed=5 * 10**6, transcendentals=0),
    )(gradient, left_basis, right_basis, first_moment, second_moment)


def solution(mesh):
    return jax.shard_map(
        body,
        mesh=mesh,
        in_specs=(
            P("wide", "narrow"),
            P(None, "narrow"),
            P("wide", "narrow"),
            P("wide", "narrow"),
            P("wide", "narrow"),
        ),
        out_specs=(P("wide", "narrow"), P("wide", "narrow"), P("wide", "narrow")),
        check_vma=False,
    )
```

```python
import jax
import jax.numpy as jnp
from jax import lax
from jax.experimental import pallas as pl
from jax.experimental.pallas import tpu as pltpu
from jax.sharding import PartitionSpec as P

STEP = 10

beta_first = 0.9
beta_second = 0.95
epsilon = 1e-08

MESH = pl.DeviceIdType.MESH
BF16 = jnp.bfloat16
F32 = jnp.float32

NY, NXL, NZ = 4, 2, 8
GROUP = NY * NXL
GROWS = 40
ROWS = 112
COLS = 1792
EIG = 640
BLOCK = NZ * GROWS
HALF = COLS // 2
BANDS = ((0, 64), (64, 48))
PIECES = (((0, 32), (32, 32)), ((0, 32), (32, 16)))
SPREAD = ((2, 1), (2, 0), (1, 1), (3, 1), (1, 0), (3, 0), (0, 1), (0, 0))
STRIPS = ((0, 256), (256, 256), (512, 384), (896, 256), (1152, 256), (1408, 384))


class Copies:
    def __init__(self, send_sem, recv_sem, local_sem):
        self.send_sem, self.recv_sem, self.local_sem = send_sem, recv_sem, local_sem
        self.made, self.here, self.waited = {}, {}, set()

    def start(self, name, src, dst, device):
        at = len(self.made)
        copy = pltpu.make_async_remote_copy(
            src_ref=src,
            dst_ref=dst,
            send_sem=self.send_sem.at[at],
            recv_sem=self.recv_sem.at[at],
            device_id=device,
            device_id_type=MESH,
        )
        copy.start()
        self.made[name] = copy

    def local(self, name, src, dst):
        copy = pltpu.make_async_copy(src, dst, self.local_sem.at[len(self.here)])
        copy.start()
        self.here[name] = copy

    def wait(self, *names):
        for name in names:
            if name not in self.waited:
                self.waited.add(name)
                if name in self.here:
                    self.here[name].wait()
                else:
                    self.made[name].wait_recv()

    def finish(self):
        self.wait(*self.here, *self.made)
        for copy in self.made.values():
            copy.wait_send()


def kernel(
    gradient, left_basis, right_basis, first_moment, second_moment,
    update, new_first, new_second,
    g_slots, g_wide, g_all, r_top, r_low, left, first, second, first_out, second_out,
    partial_top, partial_low, got_top, got_low, sent_top, sent_low, mid_top, mid_low,
    back_top, back_low, bgot_top, bgot_low, bsent_top, bsent_low, end_top, end_low,
    total, sums, sums_in, update_out,
    local_sem, send_sem, recv_sem,
):
    wide, narrow = lax.axis_index("wide"), lax.axis_index("narrow")
    y, xl, z = wide // (NXL * NZ), lax.rem(wide // NZ, NXL), lax.rem(wide, NZ)
    xh, core = narrow // 2, lax.rem(narrow, 2)
    own = wide // NZ

    def member(dy, dxl):
        return lax.rem(y + dy, NY) * NXL + lax.rem(xl + dxl, NXL)

    def source_of(dy, dxl):
        return member((NY - dy) % NY, dxl)

    def at(group=own, zz=z, hi=xh, cc=core):
        return {"wide": group * NZ + zz, "narrow": hi * 2 + cc}

    z_up, z_down = at(zz=lax.rem(z + 1, NZ)), at(zz=lax.rem(z + NZ - 1, NZ))
    y_up, y_down = at(group=member(1, 0)), at(group=member(3, 0))
    x_other = at(group=member(0, 1))
    sibling = at(cc=1 - core)
    target_hi = lax.rem(xh + core, 2)

    def target(dy, dxl):
        if (dy, dxl) == (0, 0):
            return at(hi=1 - xh)
        return at(group=member(dy, dxl), hi=target_hi)

    r_bands = (r_top, r_low)
    copies = Copies(send_sem, recv_sem, local_sem)
    for band, (first_row, rows) in enumerate(BANDS):
        copies.local(f"r{band}", right_basis.at[pl.ds(first_row, rows), :], r_bands[band].at[own])
    copies.local("g", gradient, g_slots.at[z])
    copies.local("left", left_basis, left)
    copies.local("first", first_moment, first)
    copies.local("second", second_moment, second)

    barrier = pltpu.get_barrier_semaphore()
    peers = [z_up, z_down, y_up, y_down, x_other, sibling] + [target(*d) for d in SPREAD]
    for peer in peers:
        pl.semaphore_signal(barrier, inc=1, device_id=peer, device_id_type=MESH)
    pl.semaphore_wait(barrier, len(peers))

    def send_g(hop, half):
        for way, sign, device in ((0, 1, z_up), (1, -1, z_down)):
            if hop < 3 or half == way:
                ref = g_slots.at[lax.rem(z - sign * hop + NZ, NZ), :, pl.ds(half * HALF, HALF)]
                copies.start(f"g{hop}{half}{way}", ref, ref, device)

    def pass_g(hop, half):
        for way in (0, 1):
            if hop < 3 or half == way:
                copies.wait(f"g{hop - 1}{half}{way}")
        send_g(hop, half)

    routes = {
        "+0": ((0, 0), 0, y_up, None),
        "+1": ((0, 0), 1, y_up, None),
        "-0": ((0, 0), 0, y_down, None),
        "-1": ((0, 0), 1, y_down, None),
        "x0": ((0, 0), 0, x_other, None),
        "x1": ((0, 0), 1, x_other, None),
        "++": ((3, 0), 0, y_up, "+0"),
        "--": ((1, 0), 1, y_down, "-1"),
        "fx1": ((1, 0), 0, x_other, "-0"),
        "fx3": ((3, 0), 0, x_other, "+0"),
        "y+": ((0, 1), 1, y_up, "x1"),
        "y-": ((0, 1), 1, y_down, "x1"),
        "y++": ((3, 1), 1, y_up, "y+"),
        "y--": ((1, 1), 0, y_down, "fx1"),
    }

    def pass_r(band, *names):
        for name in names:
            block, piece, device, after = routes[name]
            copies.wait(f"r{band}" if after is None else f"r{band}{after}")
            ref = r_bands[band].at[member(*block), pl.ds(*PIECES[band][piece]), :]
            copies.start(f"r{band}{name}", ref, ref, device)

    send_own = pass_r

    def compact(distance):
        slot = lax.rem(z + distance + NZ, NZ)
        g_wide[pl.ds(pl.multiple_of(slot * GROWS, 8), GROWS), :] = g_slots[slot].astype(F32)

    copies.wait("g")
    send_g(0, 0)
    send_g(0, 1)
    send_own(0, "+0", "-0", "x1", "+1", "-1", "x0")
    compact(0)
    pass_g(1, 0)
    pass_r(0, "++", "fx1", "y+", "y-", "fx3")
    send_own(1, "+0", "-0", "x1")
    pass_g(1, 1)
    send_own(1, "+1", "-1", "x0")
    pass_r(0, "--")
    compact(1)
    compact(-1)
    pass_g(2, 0)
    pass_g(2, 1)
    pass_r(0, "y--")
    compact(2)
    compact(-2)
    pass_g(3, 0)
    pass_r(0, "y++")
    pass_r(1, "fx1", "y+", "y-")
    pass_g(3, 1)
    pass_r(1, "--", "++", "fx3")
    copies.wait("g201", "g210")
    compact(3)
    compact(-3)
    copies.wait("g300", "g311")
    compact(4)
    g_all[...] = g_wide[...].astype(BF16)

    def left_rows(group):
        return left[pl.ds(pl.multiple_of(group * BLOCK, 64), BLOCK), :]

    def give_core(tag, band, i, partial, got, slots):
        copies.start(f"{tag}{band}c{i}", partial.at[slots], got.at[slots], sibling)

    def right_products(band, partial, got):
        rows = BANDS[band][1]
        copies.wait(*(f"r{band}{name}" for name in routes))
        for i in (0, 1):
            slots = pl.ds(i * GROUP // 2, GROUP // 2)
            right = r_bands[band][slots].reshape(GROUP // 2 * rows, COLS)
            partial[slots] = lax.dot_general(
                right, g_all[...], (((1,), (1,)), ((), ())), preferred_element_type=F32
            ).reshape(GROUP // 2, rows, BLOCK)
            give_core("f", band, i, partial, got, slots)

    def spread(tag, band, i, partial, got, sent, landed):
        d = SPREAD[i]
        group = member(*d)
        value = (partial[group] + got[group]).astype(BF16)
        sent[group] = value
        copies.start(f"{tag}{band}s{d}", sent.at[group], landed.at[0, own], target(*d))
        if d == (0, 0):
            landed[1, own] = value

    def spread_right(band, partial, got, sent, landed):
        copies.wait(f"f{band}c0", f"f{band}c1")
        for i in range(GROUP):
            spread("f", band, i, partial, got, sent, landed)

    def left_products(band, normalized, partial, got, sent, landed):
        for i in range(GROUP + 2):
            if i < GROUP:
                group = member(*SPREAD[i])
                partial[group] = lax.dot_general(
                    normalized, left_rows(group), (((1,), (1,)), ((), ())), preferred_element_type=F32
                )
                give_core("b", band, i, partial, got, group)
            if i >= 2:
                copies.wait(f"b{band}c{i - 2}")
                spread("b", band, i - 2, partial, got, sent, landed)

    def share(tag, band, landed):
        for d in SPREAD:
            source = source_of(*d)
            copies.wait(f"{tag}{band}s{d}")
            if d != (0, 0):
                copies.start(f"{tag}{band}r{d}", landed.at[0, source], landed.at[1, source], sibling)

    def await_share(tag, band, d):
        if d != (0, 0):
            copies.wait(f"{tag}{band}r{d}")

    first_fix = 1.0 - beta_first**STEP
    second_fix = 1.0 - beta_second**STEP

    def middle(band, landed):
        first_row, rows = BANDS[band]
        product = jnp.zeros((2 * rows, EIG), F32)
        for d in SPREAD:
            source = source_of(*d)
            await_share("f", band, d)
            product += jnp.dot(
                landed[:, source].reshape(2 * rows, BLOCK), left_rows(source), preferred_element_type=F32
            )
        rotated = product[:rows] + product[rows:]
        at_rows = pl.ds(first_row, rows)
        copies.wait("first", "second")
        next_first = beta_first * first[at_rows, :] + (1.0 - beta_first) * rotated
        next_second = beta_second * second[at_rows, :] + (1.0 - beta_second) * rotated * rotated
        first_out[at_rows, :] = next_first
        second_out[at_rows, :] = next_second
        return (next_first / first_fix / (jnp.sqrt(next_second / second_fix) + epsilon)).astype(BF16)

    def update_part(band, landed, half):
        rows = BANDS[band][1]
        right = r_bands[band][:, :, pl.ds(half * HALF, HALF)].reshape(GROUP * rows, HALF)
        return sum(
            lax.dot_general(
                landed[i].reshape(GROUP * rows, BLOCK),
                right,
                (((0,), (0,)), ((), ())),
                preferred_element_type=F32,
            )
            for i in (0, 1)
        )

    pass_r(1, "y--")
    right_products(0, partial_top, got_top)
    pass_r(1, "y++")
    spread_right(0, partial_top, got_top, sent_top, mid_top)
    right_products(1, partial_low, got_low)
    spread_right(1, partial_low, got_low, sent_low, mid_low)
    share("f", 0, mid_top)
    copies.wait("left")
    normalized = middle(0, mid_top)
    left_products(0, normalized, back_top, bgot_top, bsent_top, end_top)
    share("f", 1, mid_low)
    normalized = middle(1, mid_low)
    left_products(1, normalized, back_low, bgot_low, bsent_low, end_low)
    copies.local("new_first", first_out, new_first)
    copies.local("new_second", second_out, new_second)
    share("b", 0, end_top)
    for d in SPREAD:
        await_share("b", 0, d)
    for half in (0, 1):
        total[:, pl.ds(half * HALF, HALF)] = update_part(0, end_top, half)
    share("b", 1, end_low)
    for d in SPREAD:
        await_share("b", 1, d)
    for half in (0, 1):
        total[:, pl.ds(half * HALF, HALF)] += update_part(1, end_low, half)

    def total_rows(distance, strip):
        rows = lax.rem(z + distance + NZ, NZ) * GROWS
        return total[pl.ds(pl.multiple_of(rows, 8), GROWS), pl.ds(*STRIPS[strip])]

    for step in range(4):
        for strip in (0, 3, 1, 4, 2, 5):
            for way, sign, device in ((0, -1, z_down), (1, 1, z_up)):
                starts = strip // 3 == way
                if step == 0 and not starts:
                    continue
                columns = pl.ds(*STRIPS[strip])
                value = total_rows(sign * (4 - step), strip)
                if step > 1 or (step == 1 and starts):
                    copies.wait(f"u{step - 1}{way}{strip}")
                    value = value + sums_in[way, step - 1, :, columns].astype(F32)
                sums[way, step, :, columns] = value.astype(BF16)
                copies.start(
                    f"u{step}{way}{strip}",
                    sums.at[way, step, :, columns],
                    sums_in.at[way, step, :, columns],
                    device,
                )
    for strip in (0, 3, 1, 4, 2, 5):
        columns = pl.ds(*STRIPS[strip])
        value = total_rows(0, strip)
        for way in (0, 1):
            copies.wait(f"u3{way}{strip}")
            value = value + sums_in[way, 3, :, columns].astype(F32)
        update_out[:, columns] = value
    copies.local("update", update_out, update)
    copies.finish()


COPIES = 14 + 28 + 2 * (2 + 8 + 7) + 2 * (8 + 8 + 7) + 42


def body(gradient, left_basis, right_basis, first_moment, second_moment):
    def bands(*shape, dtype):
        return [pltpu.VMEM((*shape, rows, BLOCK), dtype) for _, rows in BANDS]

    middle = [
        *bands(GROUP, dtype=F32),
        *bands(GROUP, dtype=F32),
        *bands(GROUP, dtype=BF16),
        *bands(2, GROUP, dtype=BF16),
    ]
    moment = pltpu.VMEM((ROWS, EIG), F32)
    return pl.pallas_call(
        kernel,
        out_shape=(
            jax.ShapeDtypeStruct((GROWS, COLS), F32),
            jax.ShapeDtypeStruct((ROWS, EIG), F32),
            jax.ShapeDtypeStruct((ROWS, EIG), F32),
        ),
        in_specs=[pl.BlockSpec(memory_space=pl.ANY)] * 5,
        out_specs=[pl.BlockSpec(memory_space=pl.ANY)] * 3,
        scratch_shapes=[
            pltpu.VMEM((NZ, GROWS, COLS), BF16),
            pltpu.VMEM((BLOCK, COLS), F32),
            pltpu.VMEM((BLOCK, COLS), BF16),
            *(pltpu.VMEM((GROUP, rows, COLS), BF16) for _, rows in BANDS),
            pltpu.VMEM((GROUP * BLOCK, EIG), BF16),
            *[moment] * 4,
            *middle,
            *middle,
            pltpu.VMEM((BLOCK, COLS), F32),
            pltpu.VMEM((2, 4, GROWS, COLS), BF16),
            pltpu.VMEM((2, 4, GROWS, COLS), BF16),
            pltpu.VMEM((GROWS, COLS), F32),
            pltpu.SemaphoreType.DMA((9,)),
            pltpu.SemaphoreType.DMA((COPIES,)),
            pltpu.SemaphoreType.DMA((COPIES,)),
        ],
        compiler_params=pltpu.CompilerParams(
            collective_id=0, has_side_effects=True, vmem_limit_bytes=56 * 1024 * 1024
        ),
        cost_estimate=pl.CostEstimate(flops=3 * 10**9, bytes_accessed=5 * 10**6, transcendentals=0),
    )(gradient, left_basis, right_basis, first_moment, second_moment)


def solution(mesh):
    return jax.shard_map(
        body,
        mesh=mesh,
        in_specs=(
            P("wide", "narrow"),
            P(None, "narrow"),
            P("wide", "narrow"),
            P("wide", "narrow"),
            P("wide", "narrow"),
        ),
        out_specs=(P("wide", "narrow"), P("wide", "narrow"), P("wide", "narrow")),
        check_vma=False,
    )
```

```python
import jax
import jax.numpy as jnp
from jax import lax
from jax.experimental import pallas as pl
from jax.experimental.pallas import tpu as pltpu
from jax.sharding import PartitionSpec as P

STEP = 10

beta_first = 0.9
beta_second = 0.95
epsilon = 1e-08

MESH = pl.DeviceIdType.MESH
BF16 = jnp.bfloat16
F32 = jnp.float32

NY, NXL, NZ = 4, 2, 8
GROUP = NY * NXL
GROWS = 40
ROWS = 112
COLS = 1792
EIG = 640
BLOCK = NZ * GROWS
HALF = COLS // 2
BANDS = ((0, 64), (64, 48))
PIECES = (((0, 32), (32, 32)), ((0, 32), (32, 16)))
FAR_FIRST = (2, 1, 3, 0)
SPREAD = tuple((dy, e) for dy in FAR_FIRST for e in (1, 0))
G_STRIPS = ((0, 384), (384, 512), (896, 384), (1280, 512))
STRIPS = ((0, 256), (256, 256), (512, 384), (896, 256), (1152, 256), (1408, 384))


class Copies:
    def __init__(self, send_sem, recv_sem, local_sem):
        self.send_sem, self.recv_sem, self.local_sem = send_sem, recv_sem, local_sem
        self.made, self.here, self.waited = {}, {}, set()

    def start(self, name, src, dst, device, only=None):
        at = len(self.made)
        copy = pltpu.make_async_remote_copy(
            src_ref=src,
            dst_ref=dst,
            send_sem=self.send_sem.at[at],
            recv_sem=self.recv_sem.at[at],
            device_id=device,
            device_id_type=MESH,
        )
        self.made[name] = copy, (lambda act: act()) if only is None else pl.when(only)
        self.made[name][1](copy.start)

    def local(self, name, src, dst):
        copy = pltpu.make_async_copy(src, dst, self.local_sem.at[len(self.here)])
        copy.start()
        self.here[name] = copy

    def wait(self, *names):
        for name in names:
            if name not in self.waited:
                self.waited.add(name)
                if name in self.here:
                    self.here[name].wait()
                else:
                    copy, where = self.made[name]
                    where(copy.wait_recv)

    def finish(self):
        self.wait(*self.here, *self.made)
        for copy, where in self.made.values():
            where(copy.wait_send)


def kernel(
    gradient, left_basis, right_basis, first_moment, second_moment,
    update, new_first, new_second,
    g_slots, g_wide, g_all, r_top, r_low, left, first, second, first_out, second_out,
    keep_top, keep_low, give_top, give_low, got_top, got_low, sent_top, sent_low, mid_top, mid_low,
    bkeep_top, bkeep_low, bgive_top, bgive_low, bgot_top, bgot_low, bsent_top, bsent_low, end_top, end_low,
    total, sums, sums_in, update_out,
    local_sem, send_sem, recv_sem,
):
    wide, narrow = lax.axis_index("wide"), lax.axis_index("narrow")
    y, xl, z = wide // (NXL * NZ), lax.rem(wide // NZ, NXL), lax.rem(wide, NZ)
    xh, core = narrow // 2, lax.rem(narrow, 2)
    own = wide // NZ

    def member(dy, dxl):
        return lax.rem(y + dy, NY), lax.rem(xl + dxl, NXL)

    def at(group=(y, xl), zz=z, hi=xh, cc=core):
        return {"wide": (group[0] * NXL + group[1]) * NZ + zz, "narrow": hi * 2 + cc}

    z_up, z_down = at(zz=lax.rem(z + 1, NZ)), at(zz=lax.rem(z + NZ - 1, NZ))
    y_up, y_down = at(group=member(1, 0)), at(group=member(3, 0))
    x_other = at(group=member(0, 1))
    sibling = at(cc=1 - core)

    def target(dy, e):
        return at(group=member(dy, core), hi=lax.rem(xh + e, 2))

    r_bands = (r_top, r_low)
    copies = Copies(send_sem, recv_sem, local_sem)
    for band, (first_row, rows) in enumerate(BANDS):
        copies.local(f"r{band}", right_basis.at[pl.ds(first_row, rows), :], r_bands[band].at[y, xl])
    copies.local("g", gradient, g_slots.at[z])
    copies.local("left", left_basis, left)
    copies.local("first", first_moment, first)
    copies.local("second", second_moment, second)

    barrier = pltpu.get_barrier_semaphore()
    peers = [z_up, z_down, y_up, y_down, x_other, sibling] + [target(*d) for d in SPREAD if d != (0, 0)]
    for peer in peers:
        pl.semaphore_signal(barrier, inc=1, device_id=peer, device_id_type=MESH)
    pl.semaphore_wait(barrier, len(peers))

    def pass_g(hop, *strips):
        for strip in strips:
            for way, sign, device in ((0, 1, z_up), (1, -1, z_down)):
                if hop < 3 or strip // 2 == way:
                    copies.wait(f"g{hop - 1}{strip}{way}" if hop else "g")
                    ref = g_slots.at[lax.rem(z - sign * hop + NZ, NZ), :, pl.ds(*G_STRIPS[strip])]
                    copies.start(f"g{hop}{strip}{way}", ref, ref, device)

    def await_g(hop, ways=(0, 1)):
        copies.wait(*(f"g{hop}{strip}{way}" for strip in range(4) for way in ways if hop < 3 or strip // 2 == way))

    routes = {
        "+0": ((0, 0), 0, y_up, None),
        "+1": ((0, 0), 1, y_up, None),
        "-0": ((0, 0), 0, y_down, None),
        "-1": ((0, 0), 1, y_down, None),
        "x0": ((0, 0), 0, x_other, None),
        "x1": ((0, 0), 1, x_other, None),
        "++": ((3, 0), 0, y_up, "+0"),
        "--": ((1, 0), 1, y_down, "-1"),
        "fx1": ((1, 0), 0, x_other, "-0"),
        "fx3": ((3, 0), 0, x_other, "+0"),
        "y+": ((0, 1), 1, y_up, "x1"),
        "y-": ((0, 1), 1, y_down, "x1"),
        "y++": ((3, 1), 1, y_up, "y+"),
        "y--": ((1, 1), 0, y_down, "fx1"),
    }

    def pass_r(band, *names):
        for name in names:
            block, piece, device, after = routes[name]
            copies.wait(f"r{band}" if after is None else f"r{band}{after}")
            ref = r_bands[band].at[(*member(*block), pl.ds(*PIECES[band][piece]))]
            copies.start(f"r{band}{name}", ref, ref, device)

    send_own = pass_r

    def compact(distance):
        slot = lax.rem(z + distance + NZ, NZ)
        g_wide[pl.ds(pl.multiple_of(slot * GROWS, 8), GROWS), :] = g_slots[slot].astype(F32)

    pass_g(0, 0, 2)
    pass_r(0, "+0", "-0", "x1")
    pass_g(0, 1, 3)
    pass_r(0, "+1", "-1", "x0")
    compact(0)
    pass_g(1, 0, 2)
    pass_r(0, "++", "fx1", "y+", "y-", "fx3")
    pass_r(1, "+0", "-0", "x1")
    pass_g(1, 1, 3)
    pass_r(1, "+1", "-1", "x0")
    pass_g(2, 0, 2)
    pass_r(0, "--")
    pass_g(2, 1, 3)
    compact(1)
    compact(-1)
    pass_g(3, 0, 2)
    pass_r(0, "y--")
    pass_g(3, 1, 3)
    compact(2)
    compact(-2)
    pass_r(0, "y++")
    pass_r(1, "fx1", "y+", "y-", "--", "++", "fx3")
    await_g(2)
    compact(3)
    compact(-3)
    await_g(3)
    compact(4)
    g_all[...] = g_wide[...].astype(BF16)

    def left_rows(yy, xx):
        return left[pl.ds(pl.multiple_of((yy * NXL + xx) * BLOCK, 64), BLOCK), :]

    theirs, mine = lax.rem(xl + 1 - core, NXL), lax.rem(xl + core, NXL)

    def right_products(band, keep, give, got):
        rows = BANDS[band][1]
        copies.wait(*(f"r{band}{name}" for name in routes))
        for xx, result in ((theirs, give), (mine, keep)):
            right = r_bands[band][:, xx].reshape(NY * rows, COLS)
            result[...] = lax.dot_general(
                right, g_all[...], (((1,), (1,)), ((), ())), preferred_element_type=F32
            ).reshape(NY, rows, BLOCK)
            if result is give:
                copies.start(f"f{band}c", give, got, sibling)

    def spread(tag, band, dy, keep, got, sent, landed):
        yy = lax.rem(y + dy, NY)
        value = (keep[yy] + got[yy]).astype(BF16)
        sent[yy] = value
        for e in (1, 0):
            only = None
            if (dy, e) == (0, 0):
                only = core == 1

                @pl.when(core == 0)
                def _():
                    landed[y, xl, 0] = value

            copies.start(f"{tag}{band}s{dy}{e}", sent.at[yy], landed.at[y, xl, e], target(dy, e), only)

    def spread_right(band, keep, got, sent, landed):
        copies.wait(f"f{band}c")
        for dy in FAR_FIRST:
            spread("f", band, dy, keep, got, sent, landed)

    def left_products(band, normalized, keep, give, got, sent, landed):
        def product(yy, xx):
            return lax.dot_general(
                normalized, left_rows(yy, xx), (((1,), (1,)), ((), ())), preferred_element_type=F32
            )

        for dy in FAR_FIRST:
            yy = lax.rem(y + dy, NY)
            give[yy] = product(yy, theirs)
            copies.start(f"b{band}c{dy}", give.at[yy], got.at[yy], sibling)
        for dy in FAR_FIRST:
            yy = lax.rem(y + dy, NY)
            keep[yy] = product(yy, mine)
            copies.wait(f"b{band}c{dy}")
            spread("b", band, dy, keep, got, sent, landed)

    def share(tag, band, landed):
        for dy in FAR_FIRST:
            ref = landed.at[lax.rem(y + NY - dy, NY), mine]
            copies.wait(f"{tag}{band}s{dy}1", f"{tag}{band}s{dy}0")
            copies.start(f"{tag}{band}r{dy}", ref, ref, sibling)

    first_fix = 1.0 - beta_first**STEP
    second_fix = 1.0 - beta_second**STEP

    def middle(band, landed):
        first_row, rows = BANDS[band]
        product = jnp.zeros((2 * rows, EIG), F32)
        for xx in (mine, theirs):
            for dy in FAR_FIRST:
                yy = lax.rem(y + NY - dy, NY)
                if xx is theirs:
                    copies.wait(f"f{band}r{dy}")
                product += jnp.dot(
                    landed[yy, xx].reshape(2 * rows, BLOCK), left_rows(yy, xx), preferred_element_type=F32
                )
        rotated = product[:rows] + product[rows:]
        at_rows = pl.ds(first_row, rows)
        copies.wait("first", "second")
        next_first = beta_first * first[at_rows, :] + (1.0 - beta_first) * rotated
        next_second = beta_second * second[at_rows, :] + (1.0 - beta_second) * rotated * rotated
        first_out[at_rows, :] = next_first
        second_out[at_rows, :] = next_second
        return (next_first / first_fix / (jnp.sqrt(next_second / second_fix) + epsilon)).astype(BF16)

    def update_part(band, landed, half):
        rows = BANDS[band][1]
        right = r_bands[band][:, :, :, pl.ds(half * HALF, HALF)].reshape(GROUP * rows, HALF)
        return sum(
            lax.dot_general(
                landed[:, :, i].reshape(GROUP * rows, BLOCK),
                right,
                (((0,), (0,)), ((), ())),
                preferred_element_type=F32,
            )
            for i in (0, 1)
        )

    pass_r(1, "y--")
    right_products(0, keep_top, give_top, got_top)
    pass_r(1, "y++")
    spread_right(0, keep_top, got_top, sent_top, mid_top)
    right_products(1, keep_low, give_low, got_low)
    spread_right(1, keep_low, got_low, sent_low, mid_low)
    share("f", 0, mid_top)
    copies.wait("left")
    normalized = middle(0, mid_top)
    left_products(0, normalized, bkeep_top, bgive_top, bgot_top, bsent_top, end_top)
    share("f", 1, mid_low)
    normalized = middle(1, mid_low)
    left_products(1, normalized, bkeep_low, bgive_low, bgot_low, bsent_low, end_low)
    copies.local("new_first", first_out, new_first)
    copies.local("new_second", second_out, new_second)
    share("b", 0, end_top)
    copies.wait(*(f"b0r{dy}" for dy in FAR_FIRST))
    for half in (0, 1):
        total[:, pl.ds(half * HALF, HALF)] = update_part(0, end_top, half)
    share("b", 1, end_low)
    copies.wait(*(f"b1r{dy}" for dy in FAR_FIRST))
    for half in (0, 1):
        total[:, pl.ds(half * HALF, HALF)] += update_part(1, end_low, half)

    def total_rows(distance, strip):
        rows = lax.rem(z + distance + NZ, NZ) * GROWS
        return total[pl.ds(pl.multiple_of(rows, 8), GROWS), pl.ds(*STRIPS[strip])]

    for step in range(4):
        for strip in (0, 3, 1, 4, 2, 5):
            for way, sign, device in ((0, -1, z_down), (1, 1, z_up)):
                starts = strip // 3 == way
                if step == 0 and not starts:
                    continue
                columns = pl.ds(*STRIPS[strip])
                value = total_rows(sign * (4 - step), strip)
                if step > 1 or (step == 1 and starts):
                    copies.wait(f"u{step - 1}{way}{strip}")
                    value = value + sums_in[way, step - 1, :, columns].astype(F32)
                sums[way, step, :, columns] = value.astype(BF16)
                copies.start(
                    f"u{step}{way}{strip}",
                    sums.at[way, step, :, columns],
                    sums_in.at[way, step, :, columns],
                    device,
                )
    for strip in (0, 3, 1, 4, 2, 5):
        columns = pl.ds(*STRIPS[strip])
        value = total_rows(0, strip)
        for way in (0, 1):
            copies.wait(f"u3{way}{strip}")
            value = value + sums_in[way, 3, :, columns].astype(F32)
        update_out[:, columns] = value
    copies.local("update", update_out, update)
    copies.finish()


COPIES = 28 + 28 + 2 * (1 + 8 + 4) + 2 * (4 + 8 + 4) + 42


def body(gradient, left_basis, right_basis, first_moment, second_moment):
    def bands(*shape, dtype):
        return [pltpu.VMEM((*shape, rows, BLOCK), dtype) for _, rows in BANDS]

    middle = [
        *bands(NY, dtype=F32),
        *bands(NY, dtype=F32),
        *bands(NY, dtype=F32),
        *bands(NY, dtype=BF16),
        *bands(NY, NXL, 2, dtype=BF16),
    ]
    moment = pltpu.VMEM((ROWS, EIG), F32)
    results = pl.pallas_call(
        kernel,
        out_shape=(
            jax.ShapeDtypeStruct((GROWS, COLS), F32),
            jax.ShapeDtypeStruct((ROWS, EIG), F32),
            jax.ShapeDtypeStruct((ROWS, EIG), F32),
        ),
        in_specs=[pl.BlockSpec(memory_space=pl.ANY)] * 5,
        out_specs=[pl.BlockSpec(memory_space=pl.ANY)] * 3,
        scratch_shapes=[
            pltpu.VMEM((NZ, GROWS, COLS), BF16),
            pltpu.VMEM((BLOCK, COLS), F32),
            pltpu.VMEM((BLOCK, COLS), BF16),
            *(pltpu.VMEM((NY, NXL, rows, COLS), BF16) for _, rows in BANDS),
            pltpu.VMEM((GROUP * BLOCK, EIG), BF16),
            *[moment] * 4,
            *middle,
            *middle,
            pltpu.VMEM((BLOCK, COLS), F32),
            pltpu.VMEM((2, 4, GROWS, COLS), BF16),
            pltpu.VMEM((2, 4, GROWS, COLS), BF16),
            pltpu.VMEM((GROWS, COLS), F32),
            pltpu.SemaphoreType.DMA((9,)),
            pltpu.SemaphoreType.DMA((COPIES,)),
            pltpu.SemaphoreType.DMA((COPIES,)),
        ],
        compiler_params=pltpu.CompilerParams(
            collective_id=0, has_side_effects=True, vmem_limit_bytes=56 * 1024 * 1024
        ),
        cost_estimate=pl.CostEstimate(flops=3 * 10**9, bytes_accessed=5 * 10**6, transcendentals=0),
    )(gradient, left_basis, right_basis, first_moment, second_moment)
    return hand_over(results)


def hand_over(results):
    def move(*refs):
        sources, targets, held, sem = refs[:3], refs[3:6], refs[6:9], refs[9]
        loads = [pltpu.make_async_copy(sources[i], held[i], sem.at[i]) for i in range(3)]
        stores = [pltpu.make_async_copy(held[i], targets[i], sem.at[i + 3]) for i in range(3)]
        for one in loads:
            one.start()
        for load, store in zip(loads, stores):
            load.wait()
            store.start()
        for one in stores:
            one.wait()

    return pl.pallas_call(
        move,
        out_shape=tuple(jax.ShapeDtypeStruct(one.shape, one.dtype) for one in results),
        in_specs=[pl.BlockSpec(memory_space=pl.ANY)] * 3,
        out_specs=[pl.BlockSpec(memory_space=pl.ANY)] * 3,
        compiler_params=pltpu.CompilerParams(vmem_limit_bytes=60 * 1024 * 1024),
        scratch_shapes=[
            *(pltpu.VMEM(one.shape, one.dtype) for one in results),
            pltpu.SemaphoreType.DMA((6,)),
        ],
    )(*results)


def solution(mesh):
    return jax.shard_map(
        body,
        mesh=mesh,
        in_specs=(
            P("wide", "narrow"),
            P(None, "narrow"),
            P("wide", "narrow"),
            P("wide", "narrow"),
            P("wide", "narrow"),
        ),
        out_specs=(P("wide", "narrow"), P("wide", "narrow"), P("wide", "narrow")),
        check_vma=False,
    )
```

```python
import jax
import jax.numpy as jnp
from jax import lax
from jax.experimental import pallas as pl
from jax.experimental.pallas import tpu as pltpu
from jax.sharding import PartitionSpec as P

STEP = 10

beta_first = 0.9
beta_second = 0.95
epsilon = 1e-08

MESH = pl.DeviceIdType.MESH
BF16 = jnp.bfloat16
F32 = jnp.float32

NY, NXL, NZ = 4, 2, 8
GROUP = NY * NXL
GROWS = 40
ROWS = 112
COLS = 1792
EIG = 640
BLOCK = NZ * GROWS
HALF = COLS // 2
BANDS = ((0, 64), (64, 48))
PIECES = (((0, 32), (32, 32)), ((0, 32), (32, 16)))
FAR_FIRST = (2, 1, 3, 0)
SPREAD = tuple((dy, e) for dy in FAR_FIRST for e in (1, 0))
G_STRIPS = ((0, 384), (384, 512), (896, 384), (1280, 512))
STRIPS = ((0, 256), (256, 256), (512, 384), (896, 256), (1152, 256), (1408, 384))


class Copies:
    def __init__(self, send_sem, recv_sem, local_sem):
        self.send_sem, self.recv_sem, self.local_sem = send_sem, recv_sem, local_sem
        self.made, self.here, self.waited = {}, {}, set()

    def start(self, name, src, dst, device, only=None):
        at = len(self.made)
        copy = pltpu.make_async_remote_copy(
            src_ref=src,
            dst_ref=dst,
            send_sem=self.send_sem.at[at],
            recv_sem=self.recv_sem.at[at],
            device_id=device,
            device_id_type=MESH,
        )
        self.made[name] = copy, (lambda act: act()) if only is None else pl.when(only)
        self.made[name][1](copy.start)

    def local(self, name, src, dst):
        copy = pltpu.make_async_copy(src, dst, self.local_sem.at[len(self.here)])
        copy.start()
        self.here[name] = copy

    def wait(self, *names):
        for name in names:
            if name not in self.waited:
                self.waited.add(name)
                if name in self.here:
                    self.here[name].wait()
                else:
                    copy, where = self.made[name]
                    where(copy.wait_recv)

    def finish(self):
        self.wait(*self.here, *self.made)
        for copy, where in self.made.values():
            where(copy.wait_send)


def kernel(
    gradient, left_basis, right_basis, first_moment, second_moment,
    update, new_first, new_second,
    g_slots, g_wide, g_all, r_top, r_low, left, first, second, first_out, second_out,
    keep_top, keep_low, give_top, give_low, got_top, got_low, sent_top, sent_low, mid_top, mid_low,
    bkeep_top, bkeep_low, bgive_top, bgive_low, bgot_top, bgot_low, bsent_top, bsent_low, end_top, end_low,
    total, sums, sums_in, update_out,
    local_sem, send_sem, recv_sem,
):
    wide, narrow = lax.axis_index("wide"), lax.axis_index("narrow")
    y, xl, z = wide // (NXL * NZ), lax.rem(wide // NZ, NXL), lax.rem(wide, NZ)
    xh, core = narrow // 2, lax.rem(narrow, 2)
    own = wide // NZ

    def member(dy, dxl):
        return lax.rem(y + dy, NY), lax.rem(xl + dxl, NXL)

    def at(group=(y, xl), zz=z, hi=xh, cc=core):
        return {"wide": (group[0] * NXL + group[1]) * NZ + zz, "narrow": hi * 2 + cc}

    z_up, z_down = at(zz=lax.rem(z + 1, NZ)), at(zz=lax.rem(z + NZ - 1, NZ))
    y_up, y_down = at(group=member(1, 0)), at(group=member(3, 0))
    x_other = at(group=member(0, 1))
    sibling = at(cc=1 - core)

    def target(dy, e):
        return at(group=member(dy, core), hi=lax.rem(xh + e, 2))

    r_bands = (r_top, r_low)
    copies = Copies(send_sem, recv_sem, local_sem)
    for band, (first_row, rows) in enumerate(BANDS):
        copies.local(f"r{band}", right_basis.at[pl.ds(first_row, rows), :], r_bands[band].at[y, xl])
    copies.local("g", gradient, g_slots.at[z])
    copies.local("left", left_basis, left)
    copies.local("first", first_moment, first)
    copies.local("second", second_moment, second)

    barrier = pltpu.get_barrier_semaphore()
    peers = [z_up, z_down, y_up, y_down, x_other, sibling] + [target(*d) for d in SPREAD if d != (0, 0)]
    for peer in peers:
        pl.semaphore_signal(barrier, inc=1, device_id=peer, device_id_type=MESH)
    pl.semaphore_wait(barrier, len(peers))

    def pass_g(hop, *turns):
        for turn in turns:
            for way, sign, device in ((0, 1, z_up), (1, -1, z_down)):
                strip = (turn + 2 * way) % 4
                if hop < 3 or turn < 2:
                    copies.wait(f"g{hop - 1}{strip}{way}" if hop else "g")
                    ref = g_slots.at[lax.rem(z - sign * hop + NZ, NZ), :, pl.ds(*G_STRIPS[strip])]
                    copies.start(f"g{hop}{strip}{way}", ref, ref, device)

    def await_g(hop, ways=(0, 1)):
        copies.wait(*(f"g{hop}{strip}{way}" for strip in range(4) for way in ways if hop < 3 or strip // 2 == way))

    routes = {
        "+0": ((0, 0), 0, y_up, None),
        "+1": ((0, 0), 1, y_up, None),
        "-0": ((0, 0), 0, y_down, None),
        "-1": ((0, 0), 1, y_down, None),
        "x0": ((0, 0), 0, x_other, None),
        "x1": ((0, 0), 1, x_other, None),
        "++": ((3, 0), 0, y_up, "+0"),
        "--": ((1, 0), 1, y_down, "-1"),
        "fx1": ((1, 0), 0, x_other, "-0"),
        "fx3": ((3, 0), 0, x_other, "+0"),
        "y+": ((0, 1), 1, y_up, "x1"),
        "y-": ((0, 1), 1, y_down, "x1"),
        "y++": ((3, 1), 1, y_up, "y+"),
        "y--": ((1, 1), 0, y_down, "fx1"),
    }

    def pass_r(band, *names):
        for name in names:
            block, piece, device, after = routes[name]
            copies.wait(f"r{band}" if after is None else f"r{band}{after}")
            ref = r_bands[band].at[(*member(*block), pl.ds(*PIECES[band][piece]))]
            copies.start(f"r{band}{name}", ref, ref, device)

    send_own = pass_r

    def compact(distance):
        slot = lax.rem(z + distance + NZ, NZ)
        g_wide[pl.ds(pl.multiple_of(slot * GROWS, 8), GROWS), :] = g_slots[slot].astype(F32)

    pass_g(0, 0, 1)
    pass_r(0, "+0", "-0", "x1")
    pass_g(0, 2, 3)
    pass_r(0, "+1", "-1", "x0")
    compact(0)
    pass_g(1, 0, 1)
    pass_r(0, "++", "fx1", "y+", "y-", "fx3")
    pass_r(1, "+0", "-0", "x1")
    pass_g(1, 2, 3)
    pass_r(1, "+1", "-1", "x0")
    pass_g(2, 0, 1)
    pass_r(0, "--")
    pass_g(2, 2, 3)
    compact(1)
    compact(-1)
    pass_g(3, 0, 1)
    pass_r(0, "y--")
    compact(2)
    compact(-2)
    pass_r(0, "y++")
    pass_r(1, "fx1", "y+", "y-", "--", "++", "fx3")
    await_g(2)
    compact(3)
    compact(-3)
    await_g(3)
    compact(4)
    g_all[...] = g_wide[...].astype(BF16)

    def left_rows(yy, xx):
        return left[pl.ds(pl.multiple_of((yy * NXL + xx) * BLOCK, 64), BLOCK), :]

    theirs, mine = lax.rem(xl + 1 - core, NXL), lax.rem(xl + core, NXL)

    def right_products(band, keep, give, got):
        rows = BANDS[band][1]
        copies.wait(*(f"r{band}{name}" for name in routes))
        for xx, result in ((theirs, give), (mine, keep)):
            right = r_bands[band][:, xx].reshape(NY * rows, COLS)
            result[...] = lax.dot_general(
                right, g_all[...], (((1,), (1,)), ((), ())), preferred_element_type=F32
            ).reshape(NY, rows, BLOCK)
            if result is give:
                copies.start(f"f{band}c", give, got, sibling)

    def spread(tag, band, dy, keep, got, sent, landed):
        yy = lax.rem(y + dy, NY)
        value = (keep[yy] + got[yy]).astype(BF16)
        sent[yy] = value
        for e in (1, 0):
            only = None
            if (dy, e) == (0, 0):
                only = core == 1

                @pl.when(core == 0)
                def _():
                    landed[y, xl, 0] = value

            copies.start(f"{tag}{band}s{dy}{e}", sent.at[yy], landed.at[y, xl, e], target(dy, e), only)

    def spread_right(band, keep, got, sent, landed):
        copies.wait(f"f{band}c")
        for dy in FAR_FIRST:
            spread("f", band, dy, keep, got, sent, landed)

    def left_products(band, normalized, keep, give, got, sent, landed):
        def product(yy, xx):
            return lax.dot_general(
                normalized, left_rows(yy, xx), (((1,), (1,)), ((), ())), preferred_element_type=F32
            )

        for dy in FAR_FIRST:
            yy = lax.rem(y + dy, NY)
            give[yy] = product(yy, theirs)
            copies.start(f"b{band}c{dy}", give.at[yy], got.at[yy], sibling)
        for dy in FAR_FIRST:
            yy = lax.rem(y + dy, NY)
            keep[yy] = product(yy, mine)
            copies.wait(f"b{band}c{dy}")
            spread("b", band, dy, keep, got, sent, landed)

    def share(tag, band, landed):
        for dy in FAR_FIRST:
            ref = landed.at[lax.rem(y + NY - dy, NY), mine]
            copies.wait(f"{tag}{band}s{dy}1", f"{tag}{band}s{dy}0")
            copies.start(f"{tag}{band}r{dy}", ref, ref, sibling)

    first_fix = 1.0 - beta_first**STEP
    second_fix = 1.0 - beta_second**STEP

    def middle(band, landed):
        first_row, rows = BANDS[band]
        product = jnp.zeros((2 * rows, EIG), F32)
        for xx in (mine, theirs):
            for dy in FAR_FIRST:
                yy = lax.rem(y + NY - dy, NY)
                if xx is theirs:
                    copies.wait(f"f{band}r{dy}")
                product += jnp.dot(
                    landed[yy, xx].reshape(2 * rows, BLOCK), left_rows(yy, xx), preferred_element_type=F32
                )
        rotated = product[:rows] + product[rows:]
        at_rows = pl.ds(first_row, rows)
        copies.wait("first", "second")
        next_first = beta_first * first[at_rows, :] + (1.0 - beta_first) * rotated
        next_second = beta_second * second[at_rows, :] + (1.0 - beta_second) * rotated * rotated
        first_out[at_rows, :] = next_first
        second_out[at_rows, :] = next_second
        return (next_first / first_fix / (jnp.sqrt(next_second / second_fix) + epsilon)).astype(BF16)

    def update_part(band, landed, xx, half):
        rows = BANDS[band][1]
        right = r_bands[band][:, xx, :, pl.ds(half * HALF, HALF)]
        twice = jnp.broadcast_to(right[:, None], (NY, 2, rows, HALF)).reshape(2 * NY * rows, HALF)
        return lax.dot_general(
            landed[:, xx].reshape(2 * NY * rows, BLOCK),
            twice,
            (((0,), (0,)), ((), ())),
            preferred_element_type=F32,
        )

    pass_r(1, "y--")
    right_products(0, keep_top, give_top, got_top)
    pass_r(1, "y++")
    spread_right(0, keep_top, got_top, sent_top, mid_top)
    right_products(1, keep_low, give_low, got_low)
    spread_right(1, keep_low, got_low, sent_low, mid_low)
    share("f", 0, mid_top)
    copies.wait("left")
    normalized = middle(0, mid_top)
    left_products(0, normalized, bkeep_top, bgive_top, bgot_top, bsent_top, end_top)
    share("f", 1, mid_low)
    normalized = middle(1, mid_low)
    left_products(1, normalized, bkeep_low, bgive_low, bgot_low, bsent_low, end_low)
    copies.local("new_first", first_out, new_first)
    copies.local("new_second", second_out, new_second)
    share("b", 0, end_top)
    for half in (0, 1):
        total[:, pl.ds(half * HALF, HALF)] = update_part(0, end_top, mine, half)
    copies.wait(*(f"b0r{dy}" for dy in FAR_FIRST))
    for half in (0, 1):
        total[:, pl.ds(half * HALF, HALF)] += update_part(0, end_top, theirs, half)
    share("b", 1, end_low)
    for half in (0, 1):
        total[:, pl.ds(half * HALF, HALF)] += update_part(1, end_low, mine, half)
    copies.wait(*(f"b1r{dy}" for dy in FAR_FIRST))
    for half in (0, 1):
        total[:, pl.ds(half * HALF, HALF)] += update_part(1, end_low, theirs, half)

    def total_rows(distance, strip):
        rows = lax.rem(z + distance + NZ, NZ) * GROWS
        return total[pl.ds(pl.multiple_of(rows, 8), GROWS), pl.ds(*STRIPS[strip])]

    for step in range(4):
        for strip in (0, 3, 1, 4, 2, 5):
            for way, sign, device in ((0, -1, z_down), (1, 1, z_up)):
                starts = strip // 3 == way
                if step == 0 and not starts:
                    continue
                columns = pl.ds(*STRIPS[strip])
                value = total_rows(sign * (4 - step), strip)
                if step > 1 or (step == 1 and starts):
                    copies.wait(f"u{step - 1}{way}{strip}")
                    value = value + sums_in[way, step - 1, :, columns].astype(F32)
                sums[way, step, :, columns] = value.astype(BF16)
                copies.start(
                    f"u{step}{way}{strip}",
                    sums.at[way, step, :, columns],
                    sums_in.at[way, step, :, columns],
                    device,
                )
    for strip in (0, 3, 1, 4, 2, 5):
        columns = pl.ds(*STRIPS[strip])
        value = total_rows(0, strip)
        for way in (0, 1):
            copies.wait(f"u3{way}{strip}")
            value = value + sums_in[way, 3, :, columns].astype(F32)
        update_out[:, columns] = value
    copies.local("update", update_out, update)
    copies.finish()


COPIES = 28 + 28 + 4 * (4 + 8 + 4) + 42


def body(gradient, left_basis, right_basis, first_moment, second_moment):
    def bands(*shape, dtype):
        return [pltpu.VMEM((*shape, rows, BLOCK), dtype) for _, rows in BANDS]

    middle = [
        *bands(NY, dtype=F32),
        *bands(NY, dtype=F32),
        *bands(NY, dtype=F32),
        *bands(NY, dtype=BF16),
        *bands(NY, NXL, 2, dtype=BF16),
    ]
    moment = pltpu.VMEM((ROWS, EIG), F32)
    results = pl.pallas_call(
        kernel,
        out_shape=(
            jax.ShapeDtypeStruct((GROWS, COLS), F32),
            jax.ShapeDtypeStruct((ROWS, EIG), F32),
            jax.ShapeDtypeStruct((ROWS, EIG), F32),
        ),
        in_specs=[pl.BlockSpec(memory_space=pl.ANY)] * 5,
        out_specs=[pl.BlockSpec(memory_space=pl.ANY)] * 3,
        scratch_shapes=[
            pltpu.VMEM((NZ, GROWS, COLS), BF16),
            pltpu.VMEM((BLOCK, COLS), F32),
            pltpu.VMEM((BLOCK, COLS), BF16),
            *(pltpu.VMEM((NY, NXL, rows, COLS), BF16) for _, rows in BANDS),
            pltpu.VMEM((GROUP * BLOCK, EIG), BF16),
            *[moment] * 4,
            *middle,
            *middle,
            pltpu.VMEM((BLOCK, COLS), F32),
            pltpu.VMEM((2, 4, GROWS, COLS), BF16),
            pltpu.VMEM((2, 4, GROWS, COLS), BF16),
            pltpu.VMEM((GROWS, COLS), F32),
            pltpu.SemaphoreType.DMA((9,)),
            pltpu.SemaphoreType.DMA((COPIES,)),
            pltpu.SemaphoreType.DMA((COPIES,)),
        ],
        compiler_params=pltpu.CompilerParams(
            collective_id=0, has_side_effects=True, vmem_limit_bytes=56 * 1024 * 1024
        ),
        cost_estimate=pl.CostEstimate(flops=3 * 10**9, bytes_accessed=5 * 10**6, transcendentals=0),
    )(gradient, left_basis, right_basis, first_moment, second_moment)
    return hand_over(results)


def hand_over(results):
    def move(*refs):
        sources, targets, held, sem = refs[:3], refs[3:6], refs[6:9], refs[9]
        loads = [pltpu.make_async_copy(sources[i], held[i], sem.at[i]) for i in range(3)]
        stores = [pltpu.make_async_copy(held[i], targets[i], sem.at[i + 3]) for i in range(3)]
        for one in loads:
            one.start()
        for load, store in zip(loads, stores):
            load.wait()
            store.start()
        for one in stores:
            one.wait()

    return pl.pallas_call(
        move,
        out_shape=tuple(jax.ShapeDtypeStruct(one.shape, one.dtype) for one in results),
        in_specs=[pl.BlockSpec(memory_space=pl.ANY)] * 3,
        out_specs=[pl.BlockSpec(memory_space=pl.ANY)] * 3,
        compiler_params=pltpu.CompilerParams(vmem_limit_bytes=60 * 1024 * 1024),
        scratch_shapes=[
            *(pltpu.VMEM(one.shape, one.dtype) for one in results),
            pltpu.SemaphoreType.DMA((6,)),
        ],
    )(*results)


def solution(mesh):
    return jax.shard_map(
        body,
        mesh=mesh,
        in_specs=(
            P("wide", "narrow"),
            P(None, "narrow"),
            P("wide", "narrow"),
            P("wide", "narrow"),
            P("wide", "narrow"),
        ),
        out_specs=(P("wide", "narrow"), P("wide", "narrow"), P("wide", "narrow")),
        check_vma=False,
    )
```

```python
import jax
import jax.numpy as jnp
from jax import lax
from jax.experimental import pallas as pl
from jax.experimental.pallas import tpu as pltpu
from jax.sharding import PartitionSpec as P

STEP = 10

beta_first = 0.9
beta_second = 0.95
epsilon = 1e-08

MESH = pl.DeviceIdType.MESH
BF16 = jnp.bfloat16
F32 = jnp.float32

NY, NXL, NZ = 4, 2, 8
GROUP = NY * NXL
GROWS = 40
ROWS = 112
COLS = 1792
EIG = 640
BLOCK = NZ * GROWS
HALF = COLS // 2
BANDS = ((0, 64), (64, 48))
PIECES = (((0, 32), (32, 32)), ((0, 32), (32, 16)))
FAR_FIRST = (2, 1, 3, 0)
SPREAD = tuple((dy, e) for dy in FAR_FIRST for e in (1, 0))
G_STRIPS = ((0, 384), (384, 512), (896, 384), (1280, 512))
STRIPS = ((0, 256), (256, 256), (512, 384), (896, 256), (1152, 256), (1408, 384))


class Copies:
    def __init__(self, send_sem, recv_sem, local_sem):
        self.send_sem, self.recv_sem, self.local_sem = send_sem, recv_sem, local_sem
        self.made, self.here, self.waited = {}, {}, set()

    def start(self, name, src, dst, device, only=None):
        at = len(self.made)
        copy = pltpu.make_async_remote_copy(
            src_ref=src,
            dst_ref=dst,
            send_sem=self.send_sem.at[at],
            recv_sem=self.recv_sem.at[at],
            device_id=device,
            device_id_type=MESH,
        )
        self.made[name] = copy, (lambda act: act()) if only is None else pl.when(only)
        self.made[name][1](copy.start)

    def local(self, name, src, dst):
        copy = pltpu.make_async_copy(src, dst, self.local_sem.at[len(self.here)])
        copy.start()
        self.here[name] = copy

    def wait(self, *names):
        for name in names:
            if name not in self.waited:
                self.waited.add(name)
                if name in self.here:
                    self.here[name].wait()
                else:
                    copy, where = self.made[name]
                    where(copy.wait_recv)

    def finish(self):
        self.wait(*self.here, *self.made)
        for copy, where in self.made.values():
            where(copy.wait_send)


def kernel(
    gradient, left_basis, right_basis, first_moment, second_moment,
    update, new_first, new_second,
    g_slots, g_wide, g_all, r_top, r_low, left, first, second, first_out, second_out,
    keep_top, keep_low, give_top, give_low, got_top, got_low, sent_top, sent_low, mid_top, mid_low,
    bkeep_top, bkeep_low, bgive_top, bgive_low, bgot_top, bgot_low, bsent_top, bsent_low, end_top, end_low,
    total, sums, sums_in, last_sums, last_in, update_out,
    local_sem, send_sem, recv_sem,
):
    wide, narrow = lax.axis_index("wide"), lax.axis_index("narrow")
    y, xl, z = wide // (NXL * NZ), lax.rem(wide // NZ, NXL), lax.rem(wide, NZ)
    xh, core = narrow // 2, lax.rem(narrow, 2)
    own = wide // NZ

    def member(dy, dxl):
        return lax.rem(y + dy, NY), lax.rem(xl + dxl, NXL)

    def at(group=(y, xl), zz=z, hi=xh, cc=core):
        return {"wide": (group[0] * NXL + group[1]) * NZ + zz, "narrow": hi * 2 + cc}

    z_up, z_down = at(zz=lax.rem(z + 1, NZ)), at(zz=lax.rem(z + NZ - 1, NZ))
    y_up, y_down = at(group=member(1, 0)), at(group=member(3, 0))
    x_other = at(group=member(0, 1))
    sibling = at(cc=1 - core)

    def target(dy, e):
        return at(group=member(dy, core), hi=lax.rem(xh + e, 2))

    r_bands = (r_top, r_low)
    copies = Copies(send_sem, recv_sem, local_sem)
    for band, (first_row, rows) in enumerate(BANDS):
        copies.local(f"r{band}", right_basis.at[pl.ds(first_row, rows), :], r_bands[band].at[y, xl])
    copies.local("g", gradient, g_slots.at[z])
    copies.local("left", left_basis, left)
    copies.local("first", first_moment, first)
    copies.local("second", second_moment, second)

    barrier = pltpu.get_barrier_semaphore()
    peers = [z_up, z_down, y_up, y_down, x_other, sibling] + [target(*d) for d in SPREAD if d != (0, 0)]
    for peer in peers:
        pl.semaphore_signal(barrier, inc=1, device_id=peer, device_id_type=MESH)
    pl.semaphore_wait(barrier, len(peers))

    def pass_g(hop, *turns):
        for turn in turns:
            for way, sign, device in ((0, 1, z_up), (1, -1, z_down)):
                strip = (turn + 2 * way) % 4
                if hop < 3 or turn < 2:
                    copies.wait(f"g{hop - 1}{strip}{way}" if hop else "g")
                    ref = g_slots.at[lax.rem(z - sign * hop + NZ, NZ), :, pl.ds(*G_STRIPS[strip])]
                    copies.start(f"g{hop}{strip}{way}", ref, ref, device)

    def await_g(hop, ways=(0, 1)):
        copies.wait(*(f"g{hop}{strip}{way}" for strip in range(4) for way in ways if hop < 3 or strip // 2 == way))

    routes = {
        "+0": ((0, 0), 0, y_up, None),
        "+1": ((0, 0), 1, y_up, None),
        "-0": ((0, 0), 0, y_down, None),
        "-1": ((0, 0), 1, y_down, None),
        "x0": ((0, 0), 0, x_other, None),
        "x1": ((0, 0), 1, x_other, None),
        "++": ((3, 0), 0, y_up, "+0"),
        "--": ((1, 0), 1, y_down, "-1"),
        "fx1": ((1, 0), 0, x_other, "-0"),
        "fx3": ((3, 0), 0, x_other, "+0"),
        "y+": ((0, 1), 1, y_up, "x1"),
        "y-": ((0, 1), 1, y_down, "x1"),
        "y++": ((3, 1), 1, y_up, "y+"),
        "y--": ((1, 1), 0, y_down, "fx1"),
    }

    def pass_r(band, *names):
        for name in names:
            block, piece, device, after = routes[name]
            copies.wait(f"r{band}" if after is None else f"r{band}{after}")
            ref = r_bands[band].at[(*member(*block), pl.ds(*PIECES[band][piece]))]
            copies.start(f"r{band}{name}", ref, ref, device)

    send_own = pass_r

    def compact(distance):
        slot = lax.rem(z + distance + NZ, NZ)
        g_wide[pl.ds(pl.multiple_of(slot * GROWS, 8), GROWS), :] = g_slots[slot].astype(F32)

    pass_g(0, 0, 1)
    pass_r(0, "+0", "-0", "x1")
    pass_g(0, 2, 3)
    pass_r(0, "+1", "-1", "x0")
    compact(0)
    pass_g(1, 0, 1)
    pass_r(0, "++", "fx1", "y+", "y-", "fx3")
    pass_r(1, "+0", "-0", "x1")
    pass_g(1, 2, 3)
    pass_r(1, "+1", "-1", "x0")
    pass_g(2, 0, 1)
    pass_r(0, "--")
    pass_g(2, 2, 3)
    compact(1)
    compact(-1)
    pass_g(3, 0, 1)
    pass_r(0, "y--")
    compact(2)
    compact(-2)
    pass_r(0, "y++")
    pass_r(1, "fx1", "y+", "y-", "--", "++", "fx3")
    await_g(2)
    compact(3)
    compact(-3)
    await_g(3)
    compact(4)
    g_all[...] = g_wide[...].astype(BF16)

    def left_rows(yy, xx):
        return left[pl.ds(pl.multiple_of((yy * NXL + xx) * BLOCK, 64), BLOCK), :]

    theirs, mine = lax.rem(xl + 1 - core, NXL), lax.rem(xl + core, NXL)

    def right_products(band, keep, give, got):
        rows = BANDS[band][1]
        copies.wait(*(f"r{band}{name}" for name in routes))
        for xx, result in ((theirs, give), (mine, keep)):
            right = r_bands[band][:, xx].reshape(NY * rows, COLS)
            result[...] = lax.dot_general(
                right, g_all[...], (((1,), (1,)), ((), ())), preferred_element_type=F32
            ).reshape(NY, rows, BLOCK)
            if result is give:
                copies.start(f"f{band}c", give, got, sibling)

    def spread(tag, band, dy, keep, got, sent, landed):
        yy = lax.rem(y + dy, NY)
        value = (keep[yy] + got[yy]).astype(BF16)
        sent[yy] = value
        for e in (1, 0):
            only = None
            if (dy, e) == (0, 0):
                only = core == 1

                @pl.when(core == 0)
                def _():
                    landed[y, xl, 0] = value

            copies.start(f"{tag}{band}s{dy}{e}", sent.at[yy], landed.at[y, xl, e], target(dy, e), only)

    def spread_right(band, keep, got, sent, landed):
        copies.wait(f"f{band}c")
        for dy in FAR_FIRST:
            spread("f", band, dy, keep, got, sent, landed)

    def left_products(band, normalized, keep, give, got, sent, landed):
        def product(yy, xx):
            return lax.dot_general(
                normalized, left_rows(yy, xx), (((1,), (1,)), ((), ())), preferred_element_type=F32
            )

        for dy in FAR_FIRST:
            yy = lax.rem(y + dy, NY)
            give[yy] = product(yy, theirs)
            copies.start(f"b{band}c{dy}", give.at[yy], got.at[yy], sibling)
        for dy in FAR_FIRST:
            yy = lax.rem(y + dy, NY)
            keep[yy] = product(yy, mine)
            copies.wait(f"b{band}c{dy}")
            spread("b", band, dy, keep, got, sent, landed)

    def share(tag, band, landed):
        for dy in FAR_FIRST:
            ref = landed.at[lax.rem(y + NY - dy, NY), mine]
            copies.wait(f"{tag}{band}s{dy}1", f"{tag}{band}s{dy}0")
            copies.start(f"{tag}{band}r{dy}", ref, ref, sibling)

    first_fix = 1.0 - beta_first**STEP
    second_fix = 1.0 - beta_second**STEP

    def middle(band, landed):
        first_row, rows = BANDS[band]
        product = jnp.zeros((2 * rows, EIG), F32)
        for xx in (mine, theirs):
            for dy in FAR_FIRST:
                yy = lax.rem(y + NY - dy, NY)
                if xx is theirs:
                    copies.wait(f"f{band}r{dy}")
                product += jnp.dot(
                    landed[yy, xx].reshape(2 * rows, BLOCK), left_rows(yy, xx), preferred_element_type=F32
                )
        rotated = product[:rows] + product[rows:]
        at_rows = pl.ds(first_row, rows)
        copies.wait("first", "second")
        next_first = beta_first * first[at_rows, :] + (1.0 - beta_first) * rotated
        next_second = beta_second * second[at_rows, :] + (1.0 - beta_second) * rotated * rotated
        first_out[at_rows, :] = next_first
        second_out[at_rows, :] = next_second
        return (next_first / first_fix / (jnp.sqrt(next_second / second_fix) + epsilon)).astype(BF16)

    def update_part(band, landed, xx, half):
        rows = BANDS[band][1]
        right = r_bands[band][:, xx, :, pl.ds(half * HALF, HALF)]
        twice = jnp.broadcast_to(right[:, None], (NY, 2, rows, HALF)).reshape(2 * NY * rows, HALF)
        return lax.dot_general(
            landed[:, xx].reshape(2 * NY * rows, BLOCK),
            twice,
            (((0,), (0,)), ((), ())),
            preferred_element_type=F32,
        )

    pass_r(1, "y--")
    right_products(0, keep_top, give_top, got_top)
    pass_r(1, "y++")
    spread_right(0, keep_top, got_top, sent_top, mid_top)
    right_products(1, keep_low, give_low, got_low)
    spread_right(1, keep_low, got_low, sent_low, mid_low)
    share("f", 0, mid_top)
    copies.wait("left")
    normalized = middle(0, mid_top)
    left_products(0, normalized, bkeep_top, bgive_top, bgot_top, bsent_top, end_top)
    share("f", 1, mid_low)
    normalized = middle(1, mid_low)
    left_products(1, normalized, bkeep_low, bgive_low, bgot_low, bsent_low, end_low)
    copies.local("new_first", first_out, new_first)
    copies.local("new_second", second_out, new_second)
    share("b", 0, end_top)
    for half in (0, 1):
        total[:, pl.ds(half * HALF, HALF)] = update_part(0, end_top, mine, half)
    copies.wait(*(f"b0r{dy}" for dy in FAR_FIRST))
    for half in (0, 1):
        total[:, pl.ds(half * HALF, HALF)] += update_part(0, end_top, theirs, half)
    share("b", 1, end_low)
    for half in (0, 1):
        total[:, pl.ds(half * HALF, HALF)] += update_part(1, end_low, mine, half)
    copies.wait(*(f"b1r{dy}" for dy in FAR_FIRST))
    for half in (0, 1):
        total[:, pl.ds(half * HALF, HALF)] += update_part(1, end_low, theirs, half)

    def total_rows(distance, strip):
        rows = lax.rem(z + distance + NZ, NZ) * GROWS
        return total[pl.ds(pl.multiple_of(rows, 8), GROWS), pl.ds(*STRIPS[strip])]

    for step in range(4):
        for strip in (0, 3, 1, 4, 2, 5):
            for way, sign, device in ((0, -1, z_down), (1, 1, z_up)):
                starts = strip // 3 == way
                if step == 0 and not starts:
                    continue
                columns = pl.ds(*STRIPS[strip])
                value = total_rows(sign * (4 - step), strip)
                if step > 1 or (step == 1 and starts):
                    copies.wait(f"u{step - 1}{way}{strip}")
                    value = value + sums_in[way, step - 1, :, columns].astype(F32)
                sent, landed = (last_sums, last_in) if step == 3 else (sums.at[:, step], sums_in.at[:, step])
                sent[way, :, columns] = value.astype(sent.dtype)
                copies.start(
                    f"u{step}{way}{strip}",
                    sent.at[way, :, columns],
                    landed.at[way, :, columns],
                    device,
                )
    for strip in (0, 3, 1, 4, 2, 5):
        columns = pl.ds(*STRIPS[strip])
        value = total_rows(0, strip)
        for way in (0, 1):
            copies.wait(f"u3{way}{strip}")
            value = value + last_in[way, :, columns]
        update_out[:, columns] = value
        copies.local(f"update{strip}", update_out.at[:, columns], update.at[:, columns])
    copies.finish()


COPIES = 28 + 28 + 4 * (4 + 8 + 4) + 42


def body(gradient, left_basis, right_basis, first_moment, second_moment):
    def bands(*shape, dtype):
        return [pltpu.VMEM((*shape, rows, BLOCK), dtype) for _, rows in BANDS]

    middle = [
        *bands(NY, dtype=F32),
        *bands(NY, dtype=F32),
        *bands(NY, dtype=F32),
        *bands(NY, dtype=BF16),
        *bands(NY, NXL, 2, dtype=BF16),
    ]
    moment = pltpu.VMEM((ROWS, EIG), F32)
    results = pl.pallas_call(
        kernel,
        out_shape=(
            jax.ShapeDtypeStruct((GROWS, COLS), F32),
            jax.ShapeDtypeStruct((ROWS, EIG), F32),
            jax.ShapeDtypeStruct((ROWS, EIG), F32),
        ),
        in_specs=[pl.BlockSpec(memory_space=pl.ANY)] * 5,
        out_specs=[pl.BlockSpec(memory_space=pl.ANY)] * 3,
        scratch_shapes=[
            pltpu.VMEM((NZ, GROWS, COLS), BF16),
            pltpu.VMEM((BLOCK, COLS), F32),
            pltpu.VMEM((BLOCK, COLS), BF16),
            *(pltpu.VMEM((NY, NXL, rows, COLS), BF16) for _, rows in BANDS),
            pltpu.VMEM((GROUP * BLOCK, EIG), BF16),
            *[moment] * 4,
            *middle,
            *middle,
            pltpu.VMEM((BLOCK, COLS), F32),
            pltpu.VMEM((2, 3, GROWS, COLS), BF16),
            pltpu.VMEM((2, 3, GROWS, COLS), BF16),
            pltpu.VMEM((2, GROWS, COLS), F32),
            pltpu.VMEM((2, GROWS, COLS), F32),
            pltpu.VMEM((GROWS, COLS), F32),
            pltpu.SemaphoreType.DMA((14,)),
            pltpu.SemaphoreType.DMA((COPIES,)),
            pltpu.SemaphoreType.DMA((COPIES,)),
        ],
        compiler_params=pltpu.CompilerParams(
            collective_id=0, has_side_effects=True, vmem_limit_bytes=56 * 1024 * 1024
        ),
        cost_estimate=pl.CostEstimate(flops=3 * 10**9, bytes_accessed=5 * 10**6, transcendentals=0),
    )(gradient, left_basis, right_basis, first_moment, second_moment)
    return hand_over(results)


def hand_over(results):
    def move(*refs):
        sources, targets, held, sem = refs[:3], refs[3:6], refs[6:9], refs[9]
        loads = [pltpu.make_async_copy(sources[i], held[i], sem.at[i]) for i in range(3)]
        stores = [pltpu.make_async_copy(held[i], targets[i], sem.at[i + 3]) for i in range(3)]
        for one in loads:
            one.start()
        for load, store in zip(loads, stores):
            load.wait()
            store.start()
        for one in stores:
            one.wait()

    return pl.pallas_call(
        move,
        out_shape=tuple(jax.ShapeDtypeStruct(one.shape, one.dtype) for one in results),
        in_specs=[pl.BlockSpec(memory_space=pl.ANY)] * 3,
        out_specs=[pl.BlockSpec(memory_space=pl.ANY)] * 3,
        compiler_params=pltpu.CompilerParams(vmem_limit_bytes=60 * 1024 * 1024),
        scratch_shapes=[
            *(pltpu.VMEM(one.shape, one.dtype) for one in results),
            pltpu.SemaphoreType.DMA((6,)),
        ],
    )(*results)


def solution(mesh):
    return jax.shard_map(
        body,
        mesh=mesh,
        in_specs=(
            P("wide", "narrow"),
            P(None, "narrow"),
            P("wide", "narrow"),
            P("wide", "narrow"),
            P("wide", "narrow"),
        ),
        out_specs=(P("wide", "narrow"), P("wide", "narrow"), P("wide", "narrow")),
        check_vma=False,
    )
```

```python
import jax
import jax.numpy as jnp
from jax import lax
from jax.experimental import pallas as pl
from jax.experimental.pallas import tpu as pltpu
from jax.sharding import PartitionSpec as P

STEP = 10

beta_first = 0.9
beta_second = 0.95
epsilon = 1e-08

MESH = pl.DeviceIdType.MESH
BF16 = jnp.bfloat16
F32 = jnp.float32

NY, NXL, NZ = 4, 2, 8
GROUP = NY * NXL
GROWS = 40
ROWS = 112
COLS = 1792
EIG = 640
BLOCK = NZ * GROWS
HALF = COLS // 2
BANDS = ((0, 64), (64, 48))
PIECES = (((0, 32), (32, 32)), ((0, 32), (32, 16)))
FAR_FIRST = (2, 1, 3, 0)
SPREAD = tuple((dy, e) for dy in FAR_FIRST for e in (1, 0))
G_STRIPS = ((0, 384), (384, 512), (896, 384), (1280, 512))
STRIPS = ((0, 256), (256, 256), (512, 384), (896, 256), (1152, 256), (1408, 384))


class Copies:
    def __init__(self, send_sem, recv_sem, local_sem):
        self.send_sem, self.recv_sem, self.local_sem = send_sem, recv_sem, local_sem
        self.made, self.here, self.waited = {}, {}, set()

    def start(self, name, src, dst, device, only=None):
        at = len(self.made)
        copy = pltpu.make_async_remote_copy(
            src_ref=src,
            dst_ref=dst,
            send_sem=self.send_sem.at[at],
            recv_sem=self.recv_sem.at[at],
            device_id=device,
            device_id_type=MESH,
        )
        self.made[name] = copy, (lambda act: act()) if only is None else pl.when(only)
        self.made[name][1](copy.start)

    def local(self, name, src, dst):
        copy = pltpu.make_async_copy(src, dst, self.local_sem.at[len(self.here)])
        copy.start()
        self.here[name] = copy

    def wait(self, *names):
        for name in names:
            if name not in self.waited:
                self.waited.add(name)
                if name in self.here:
                    self.here[name].wait()
                else:
                    copy, where = self.made[name]
                    where(copy.wait_recv)

    def finish(self):
        self.wait(*self.here, *self.made)
        for copy, where in self.made.values():
            where(copy.wait_send)


def kernel(
    gradient, left_basis, right_basis, first_moment, second_moment,
    update, new_first, new_second,
    g_slots, g_wide, g_all, r_top, r_low, left, first, second, first_out, second_out,
    keep_top, keep_low, give_top, give_low, got_top, got_low, sent_top, sent_low, mid_top, mid_low,
    bkeep_top, bkeep_low, bgive_top, bgive_low, bgot_top, bgot_low, bsent_top, bsent_low, end_top, end_low,
    total, sums, sums_in, update_out,
    local_sem, send_sem, recv_sem,
):
    wide, narrow = lax.axis_index("wide"), lax.axis_index("narrow")
    y, xl, z = wide // (NXL * NZ), lax.rem(wide // NZ, NXL), lax.rem(wide, NZ)
    xh, core = narrow // 2, lax.rem(narrow, 2)
    own = wide // NZ

    def member(dy, dxl):
        return lax.rem(y + dy, NY), lax.rem(xl + dxl, NXL)

    def at(group=(y, xl), zz=z, hi=xh, cc=core):
        return {"wide": (group[0] * NXL + group[1]) * NZ + zz, "narrow": hi * 2 + cc}

    z_up, z_down = at(zz=lax.rem(z + 1, NZ)), at(zz=lax.rem(z + NZ - 1, NZ))
    y_up, y_down = at(group=member(1, 0)), at(group=member(3, 0))
    x_other = at(group=member(0, 1))
    sibling = at(cc=1 - core)

    def target(dy, e):
        return at(group=member(dy, core), hi=lax.rem(xh + e, 2))

    r_bands = (r_top, r_low)
    copies = Copies(send_sem, recv_sem, local_sem)
    for band, (first_row, rows) in enumerate(BANDS):
        copies.local(f"r{band}", right_basis.at[pl.ds(first_row, rows), :], r_bands[band].at[y, xl])
    copies.local("g", gradient, g_slots.at[z])
    copies.local("left", left_basis, left)
    copies.local("first", first_moment, first)
    copies.local("second", second_moment, second)

    barrier = pltpu.get_barrier_semaphore()
    peers = [z_up, z_down, y_up, y_down, x_other, sibling] + [target(*d) for d in SPREAD if d != (0, 0)]
    for peer in peers:
        pl.semaphore_signal(barrier, inc=1, device_id=peer, device_id_type=MESH)
    pl.semaphore_wait(barrier, len(peers))

    def pass_g(hop, *turns):
        for turn in turns:
            for way, sign, device in ((0, 1, z_up), (1, -1, z_down)):
                strip = (turn + 2 * way) % 4
                if hop < 3 or turn < 2:
                    copies.wait(f"g{hop - 1}{strip}{way}" if hop else "g")
                    ref = g_slots.at[lax.rem(z - sign * hop + NZ, NZ), :, pl.ds(*G_STRIPS[strip])]
                    copies.start(f"g{hop}{strip}{way}", ref, ref, device)

    def await_g(hop, ways=(0, 1)):
        copies.wait(*(f"g{hop}{strip}{way}" for strip in range(4) for way in ways if hop < 3 or strip // 2 == way))

    routes = {
        "+0": ((0, 0), 0, y_up, None),
        "+1": ((0, 0), 1, y_up, None),
        "-0": ((0, 0), 0, y_down, None),
        "-1": ((0, 0), 1, y_down, None),
        "x0": ((0, 0), 0, x_other, None),
        "x1": ((0, 0), 1, x_other, None),
        "++": ((3, 0), 0, y_up, "+0"),
        "--": ((1, 0), 1, y_down, "-1"),
        "fx1": ((1, 0), 0, x_other, "-0"),
        "fx3": ((3, 0), 0, x_other, "+0"),
        "y+": ((0, 1), 1, y_up, "x1"),
        "y-": ((0, 1), 1, y_down, "x1"),
        "y++": ((3, 1), 1, y_up, "y+"),
        "y--": ((1, 1), 0, y_down, "fx1"),
    }

    def pass_r(band, *names):
        for name in names:
            block, piece, device, after = routes[name]
            copies.wait(f"r{band}" if after is None else f"r{band}{after}")
            ref = r_bands[band].at[(*member(*block), pl.ds(*PIECES[band][piece]))]
            copies.start(f"r{band}{name}", ref, ref, device)

    send_own = pass_r

    def compact(distance):
        slot = lax.rem(z + distance + NZ, NZ)
        g_wide[pl.ds(pl.multiple_of(slot * GROWS, 8), GROWS), :] = g_slots[slot].astype(F32)

    pass_g(0, 0, 1)
    pass_r(0, "+0", "-0", "x1")
    pass_g(0, 2, 3)
    pass_r(0, "+1", "-1", "x0")
    compact(0)
    pass_g(1, 0, 1)
    pass_r(0, "++", "fx1", "y+", "y-", "fx3")
    pass_r(1, "+0", "-0", "x1")
    pass_g(1, 2, 3)
    pass_r(1, "+1", "-1", "x0")
    pass_g(2, 0, 1)
    pass_r(0, "--")
    pass_g(2, 2, 3)
    compact(1)
    compact(-1)
    pass_g(3, 0, 1)
    pass_r(0, "y--")
    compact(2)
    compact(-2)
    pass_r(0, "y++")
    pass_r(1, "fx1", "y+", "y-", "--", "++", "fx3")
    await_g(2)
    compact(3)
    compact(-3)
    await_g(3)
    compact(4)
    g_all[...] = g_wide[...].astype(BF16)

    def left_rows(yy, xx):
        return left[pl.ds(pl.multiple_of((yy * NXL + xx) * BLOCK, 64), BLOCK), :]

    theirs, mine = lax.rem(xl + 1 - core, NXL), lax.rem(xl + core, NXL)

    def right_products(band, keep, give, got):
        rows = BANDS[band][1]
        copies.wait(*(f"r{band}{name}" for name in routes))
        for xx, result in ((theirs, give), (mine, keep)):
            right = r_bands[band][:, xx].reshape(NY * rows, COLS)
            result[...] = lax.dot_general(
                right, g_all[...], (((1,), (1,)), ((), ())), preferred_element_type=F32
            ).reshape(NY, rows, BLOCK)
            if result is give:
                copies.start(f"f{band}c", give, got, sibling)

    def spread(tag, band, dy, keep, got, sent, landed):
        yy = lax.rem(y + dy, NY)
        value = (keep[yy] + got[yy]).astype(BF16)
        sent[yy] = value
        for e in (1, 0):
            only = None
            if (dy, e) == (0, 0):
                only = core == 1

                @pl.when(core == 0)
                def _():
                    landed[y, xl, 0] = value

            copies.start(f"{tag}{band}s{dy}{e}", sent.at[yy], landed.at[y, xl, e], target(dy, e), only)

    def spread_right(band, keep, got, sent, landed):
        copies.wait(f"f{band}c")
        for dy in FAR_FIRST:
            spread("f", band, dy, keep, got, sent, landed)

    def left_products(band, normalized, keep, give, got, sent, landed):
        def product(yy, xx):
            return lax.dot_general(
                normalized, left_rows(yy, xx), (((1,), (1,)), ((), ())), preferred_element_type=F32
            )

        for dy in FAR_FIRST:
            yy = lax.rem(y + dy, NY)
            give[yy] = product(yy, theirs)
            copies.start(f"b{band}c{dy}", give.at[yy], got.at[yy], sibling)
        for dy in FAR_FIRST:
            yy = lax.rem(y + dy, NY)
            keep[yy] = product(yy, mine)
            copies.wait(f"b{band}c{dy}")
            spread("b", band, dy, keep, got, sent, landed)

    def share(tag, band, landed):
        for dy in FAR_FIRST:
            ref = landed.at[lax.rem(y + NY - dy, NY), mine]
            copies.wait(f"{tag}{band}s{dy}1", f"{tag}{band}s{dy}0")
            copies.start(f"{tag}{band}r{dy}", ref, ref, sibling)

    first_fix = 1.0 - beta_first**STEP
    second_fix = 1.0 - beta_second**STEP

    def middle(band, landed):
        first_row, rows = BANDS[band]
        product = jnp.zeros((2 * rows, EIG), F32)
        for xx in (mine, theirs):
            for dy in FAR_FIRST:
                yy = lax.rem(y + NY - dy, NY)
                if xx is theirs:
                    copies.wait(f"f{band}r{dy}")
                product += jnp.dot(
                    landed[yy, xx].reshape(2 * rows, BLOCK), left_rows(yy, xx), preferred_element_type=F32
                )
        rotated = product[:rows] + product[rows:]
        at_rows = pl.ds(first_row, rows)
        copies.wait("first", "second")
        next_first = beta_first * first[at_rows, :] + (1.0 - beta_first) * rotated
        next_second = beta_second * second[at_rows, :] + (1.0 - beta_second) * rotated * rotated
        first_out[at_rows, :] = next_first
        second_out[at_rows, :] = next_second
        return (next_first / first_fix / (jnp.sqrt(next_second / second_fix) + epsilon)).astype(BF16)

    def update_part(band, landed, xx, half):
        rows = BANDS[band][1]
        right = r_bands[band][:, xx, :, pl.ds(half * HALF, HALF)]
        twice = jnp.broadcast_to(right[:, None], (NY, 2, rows, HALF)).reshape(2 * NY * rows, HALF)
        return lax.dot_general(
            landed[:, xx].reshape(2 * NY * rows, BLOCK),
            twice,
            (((0,), (0,)), ((), ())),
            preferred_element_type=F32,
        )

    pass_r(1, "y--")
    right_products(0, keep_top, give_top, got_top)
    pass_r(1, "y++")
    spread_right(0, keep_top, got_top, sent_top, mid_top)
    right_products(1, keep_low, give_low, got_low)
    spread_right(1, keep_low, got_low, sent_low, mid_low)
    share("f", 0, mid_top)
    copies.wait("left")
    normalized = middle(0, mid_top)
    left_products(0, normalized, bkeep_top, bgive_top, bgot_top, bsent_top, end_top)
    share("f", 1, mid_low)
    normalized = middle(1, mid_low)
    left_products(1, normalized, bkeep_low, bgive_low, bgot_low, bsent_low, end_low)
    copies.local("new_first", first_out, new_first)
    copies.local("new_second", second_out, new_second)
    share("b", 0, end_top)
    for half in (0, 1):
        total[:, pl.ds(half * HALF, HALF)] = update_part(0, end_top, mine, half)
    copies.wait(*(f"b0r{dy}" for dy in FAR_FIRST))
    for half in (0, 1):
        total[:, pl.ds(half * HALF, HALF)] += update_part(0, end_top, theirs, half)
    share("b", 1, end_low)
    for half in (0, 1):
        total[:, pl.ds(half * HALF, HALF)] += update_part(1, end_low, mine, half)
    copies.wait(*(f"b1r{dy}" for dy in FAR_FIRST))
    for half in (0, 1):
        total[:, pl.ds(half * HALF, HALF)] += update_part(1, end_low, theirs, half)

    def total_rows(distance, strip):
        rows = lax.rem(z + distance + NZ, NZ) * GROWS
        return total[pl.ds(pl.multiple_of(rows, 8), GROWS), pl.ds(*STRIPS[strip])]

    for step in range(4):
        for strip in (0, 3, 1, 4, 2, 5):
            for way, sign, device in ((0, -1, z_down), (1, 1, z_up)):
                starts = strip // 3 == way
                if step == 0 and not starts:
                    continue
                columns = pl.ds(*STRIPS[strip])
                value = total_rows(sign * (4 - step), strip)
                if step > 1 or (step == 1 and starts):
                    copies.wait(f"u{step - 1}{way}{strip}")
                    value = value + sums_in[way, step - 1, :, columns].astype(F32)
                sums[way, step, :, columns] = value.astype(BF16)
                copies.start(
                    f"u{step}{way}{strip}",
                    sums.at[way, step, :, columns],
                    sums_in.at[way, step, :, columns],
                    device,
                )
    for strip in (0, 3, 1, 4, 2, 5):
        columns = pl.ds(*STRIPS[strip])
        value = total_rows(0, strip)
        for way in (0, 1):
            copies.wait(f"u3{way}{strip}")
            value = value + sums_in[way, 3, :, columns].astype(F32)
        update_out[:, columns] = value
        copies.local(f"update{strip}", update_out.at[:, columns], update.at[:, columns])
    copies.finish()


COPIES = 28 + 28 + 4 * (4 + 8 + 4) + 42


def body(gradient, left_basis, right_basis, first_moment, second_moment):
    def bands(*shape, dtype):
        return [pltpu.VMEM((*shape, rows, BLOCK), dtype) for _, rows in BANDS]

    middle = [
        *bands(NY, dtype=F32),
        *bands(NY, dtype=F32),
        *bands(NY, dtype=F32),
        *bands(NY, dtype=BF16),
        *bands(NY, NXL, 2, dtype=BF16),
    ]
    moment = pltpu.VMEM((ROWS, EIG), F32)
    results = pl.pallas_call(
        kernel,
        out_shape=(
            jax.ShapeDtypeStruct((GROWS, COLS), F32),
            jax.ShapeDtypeStruct((ROWS, EIG), F32),
            jax.ShapeDtypeStruct((ROWS, EIG), F32),
        ),
        in_specs=[pl.BlockSpec(memory_space=pl.ANY)] * 5,
        out_specs=[pl.BlockSpec(memory_space=pl.ANY)] * 3,
        scratch_shapes=[
            pltpu.VMEM((NZ, GROWS, COLS), BF16),
            pltpu.VMEM((BLOCK, COLS), F32),
            pltpu.VMEM((BLOCK, COLS), BF16),
            *(pltpu.VMEM((NY, NXL, rows, COLS), BF16) for _, rows in BANDS),
            pltpu.VMEM((GROUP * BLOCK, EIG), BF16),
            *[moment] * 4,
            *middle,
            *middle,
            pltpu.VMEM((BLOCK, COLS), F32),
            pltpu.VMEM((2, 4, GROWS, COLS), BF16),
            pltpu.VMEM((2, 4, GROWS, COLS), BF16),
            pltpu.VMEM((GROWS, COLS), F32),
            pltpu.SemaphoreType.DMA((14,)),
            pltpu.SemaphoreType.DMA((COPIES,)),
            pltpu.SemaphoreType.DMA((COPIES,)),
        ],
        compiler_params=pltpu.CompilerParams(
            collective_id=0, has_side_effects=True, vmem_limit_bytes=56 * 1024 * 1024
        ),
        cost_estimate=pl.CostEstimate(flops=3 * 10**9, bytes_accessed=5 * 10**6, transcendentals=0),
    )(gradient, left_basis, right_basis, first_moment, second_moment)
    return hand_over(results)


def hand_over(results):
    def move(*refs):
        sources, targets, held, sem = refs[:3], refs[3:6], refs[6:9], refs[9]
        loads = [pltpu.make_async_copy(sources[i], held[i], sem.at[i]) for i in range(3)]
        stores = [pltpu.make_async_copy(held[i], targets[i], sem.at[i + 3]) for i in range(3)]
        for one in loads:
            one.start()
        for load, store in zip(loads, stores):
            load.wait()
            store.start()
        for one in stores:
            one.wait()

    return pl.pallas_call(
        move,
        out_shape=tuple(jax.ShapeDtypeStruct(one.shape, one.dtype) for one in results),
        in_specs=[pl.BlockSpec(memory_space=pl.ANY)] * 3,
        out_specs=[pl.BlockSpec(memory_space=pl.ANY)] * 3,
        compiler_params=pltpu.CompilerParams(vmem_limit_bytes=60 * 1024 * 1024),
        scratch_shapes=[
            *(pltpu.VMEM(one.shape, one.dtype) for one in results),
            pltpu.SemaphoreType.DMA((6,)),
        ],
    )(*results)


def solution(mesh):
    return jax.shard_map(
        body,
        mesh=mesh,
        in_specs=(
            P("wide", "narrow"),
            P(None, "narrow"),
            P("wide", "narrow"),
            P("wide", "narrow"),
            P("wide", "narrow"),
        ),
        out_specs=(P("wide", "narrow"), P("wide", "narrow"), P("wide", "narrow")),
        check_vma=False,
    )
```
